256 devices in a mesh: gx: 32 (over y, z_lo, core), gy: 8 (over z_hi, x).
Axes of the slice: x: 4, y: 4, z: 8 (z_hi: 2, z_lo: 4; z = z_hi * 4 + z_lo), core: 2. Of those that a mesh axis runs over, the one named last changes fastest.
Arguments:
- populations: float32 [19, 128, 256, 128], P(None, 'gx', 'gy'), may hold values from 0.02 to 0.1
- grain_position: float32 [3, 8192], P(None, 'gx'), may hold values from -6 to 6
- grain_motion: float32 [6, 8192], P(None, 'gx'), may hold values from -0.6 to 0.6
- marker_grain: int32 [524288], P(('gx', 'gy')), may hold values from 0 to 255
- marker_offset: float32 [3, 524288], P(None, ('gx', 'gy')), may hold values from -3 to 3
- marker_weights: float32 [8, 524288], P(None, ('gx', 'gy')), may hold values from 0 to 1, as said below
- marker_cell: int32 [524288], P(('gx', 'gy')), may hold values from 0 to 12158, as said below
- block_dest: int32 [4096], P(('gx', 'gy')), may hold values from 0 to 31, as said below
- bond_pairs: int32 [2, 16384], P(None, 'gx'), may hold values from 0 to 255
- bond_rest: float32 [3, 16384], P(None, 'gx'), may hold values from -6 to 6
Outputs:
- populations_next: float32 [19, 128, 256, 128], P(None, 'gx', 'gy')
- grain_load: float32 [6, 8192], P(None, 'gx')
The draws below stay inside these ranges and needn't reach their ends.
Inputs may be any that keep to these rules, and one draw needn't show every extreme that they name: A block's markers lie in the fluid brick of gx index block_dest and of the sending device's gy index; no device sends more than 2 of its blocks to one brick. marker_cell = x * 32 * 128 + y * 128 + z with x <= 2, y <= 30, z <= 126, so that the marker's 2 x 2 x 2 stencil lies inside its destination brick. `marker_weights`: each marker's eight weights are nonnegative and sum to one.
All inputs are finite; a program needn't handle non-finite values.
Results may differ from the reference program's by a relative error of at most 0.0003.
Values sent between devices are 32-bit elements; how exact they have to be, the bound alone decides.
No kernel may reach another device: no remote copies, remote signals or barrier semaphores. Data moves between devices by JAX's collectives and lax.ppermute only.
A program may use at most 128 MiB of HBM per device.

```python
import jax
import jax.numpy as jnp
from jax import lax

CX = 4
CY = 32
CZ = 128
Q = 19
MARKS = 128
CAPB = 2
BLK_DEV = 16
GR_SLAB = 256
BOND_SLAB = 512
NX = 128
NY = 256
NZ = 128
GRAINS = 8192
BONDS = 16384
MARKERS = 524288
N_GX = 32
N_GY = 8
DEVICES = 256


def draw_marker_weights(key, part):
    key = jax.random.fold_in(key, 11)
    fraction = jax.random.uniform(key, (3, MARKERS), jnp.float32)
    rows = []
    for step_x in (0, 1):
        for step_y in (0, 1):
            for step_z in (0, 1):
                factor_x = fraction[0] if step_x else 1.0 - fraction[0]
                factor_y = fraction[1] if step_y else 1.0 - fraction[1]
                factor_z = fraction[2] if step_z else 1.0 - fraction[2]
                rows.append(factor_x * factor_y * factor_z)
    return jnp.stack(rows).astype(jnp.float32)


def draw_marker_cell(key, part):
    key = jax.random.fold_in(key, 12)
    key_x, key_y, key_z = jax.random.split(key, 3)
    place_x = jax.random.randint(key_x, (MARKERS,), 0, CX - 1)
    place_y = jax.random.randint(key_y, (MARKERS,), 0, CY - 1)
    place_z = jax.random.randint(key_z, (MARKERS,), 0, CZ - 1)
    return ((place_x * CY + place_y) * CZ + place_z).astype(jnp.int32)


def draw_block_dest(key, part):
    key = jax.random.fold_in(key, 13)
    key_hot, key_rows = jax.random.split(key)
    hot_brick = jax.random.randint(key_hot, (), 0, N_GX)
    spread = (hot_brick + 1 + jnp.arange((N_GX - 1) * CAPB, dtype=jnp.int32) // CAPB) % N_GX

    def one_device(device_key):
        key_pick, key_order = jax.random.split(device_key)
        picked = jax.random.permutation(key_pick, spread)[:BLK_DEV - CAPB]
        device_row = jnp.concatenate([jnp.full((CAPB,), hot_brick, jnp.int32), picked.astype(jnp.int32)])
        return jax.random.permutation(key_order, device_row)
    return jax.vmap(one_device)(jax.random.split(key_rows, DEVICES)).reshape(-1).astype(jnp.int32)


def set_ends(values, rng, smallest, top_value):
    shape = values.shape
    index_at = [jax.random.randint(jax.random.fold_in(rng, axis), (), 0, shape[axis]) for axis in range(len(shape))]
    values = values.at[tuple(index_at)].set(smallest)
    longest = shape.index(max(shape))
    index_at[longest] = (index_at[longest] + 1) % shape[longest]
    return values.at[tuple(index_at)].set(top_value)


def steps_of(key, dims, shards, smallest, largest):
    factor_of = 1.0
    for position, shards_of in shards:
        draws = jax.random.uniform(jax.random.fold_in(jax.random.fold_in(key, 6), position), (shards_of,), jnp.float32, smallest / len(shards), largest / len(shards))
        factor_of = factor_of * jnp.repeat(jnp.exp(draws), dims[position] // shards_of).reshape((-1,) + (1,) * (len(dims) - 1 - position))
    return factor_of


def normal_values(stream_key, extent, scale, limit, cuts=(), held_as=jnp.bfloat16):
    gain = steps_of(stream_key, extent, cuts, -0.22, 0.18) if cuts else 1.0
    values = jax.random.normal(stream_key, extent, jnp.float32) * scale * gain
    return jnp.minimum(jnp.maximum(values, -limit), limit).astype(held_as)


def setup_inputs(seed: int = 0) -> dict:
    splits = jax.random.split(jax.random.key(seed), 11)
    populations = jnp.clip(0.02 + 0.08 * jax.random.uniform(splits[0], (Q, NX, NY, NZ), jnp.float32) ** steps_of(splits[0], (Q, NX, NY, NZ), ((1, 32), (2, 8)), -0.2, 0.2), 0.02, 0.1)
    grain_position = normal_values(splits[1], (3, GRAINS), 1.0, 6.0, ((1, 32),), jnp.float32)
    grain_motion = normal_values(splits[2], (6, GRAINS), 0.1, 0.6, ((1, 32),), jnp.float32)
    marker_grain = set_ends(jax.random.randint(splits[3], (MARKERS,), 0, GR_SLAB), jax.random.fold_in(splits[3], 1), 0, GR_SLAB - 1).astype(jnp.int32)
    marker_offset = normal_values(splits[4], (3, MARKERS), 0.5, 3.0, ((1, 256),), jnp.float32)
    marker_weights = draw_marker_weights(jax.random.fold_in(splits[10], 71), 0)
    marker_cell = draw_marker_cell(jax.random.fold_in(splits[10], 71), 0)
    block_dest = draw_block_dest(jax.random.fold_in(splits[10], 71), 0)
    bond_pairs = set_ends(jax.random.randint(splits[8], (2, BONDS), 0, GR_SLAB), jax.random.fold_in(splits[8], 1), 0, GR_SLAB - 1).astype(jnp.int32)
    bond_rest = normal_values(splits[9], (3, BONDS), 1.0, 6.0, ((1, 32),), jnp.float32)
    return dict(populations=populations, grain_position=grain_position, grain_motion=grain_motion, marker_grain=marker_grain, marker_offset=marker_offset, marker_weights=marker_weights, marker_cell=marker_cell, block_dest=block_dest, bond_pairs=bond_pairs, bond_rest=bond_rest)


LATTICE = ((0, 0, 0), (1, 0, 0), (-1, 0, 0), (0, 1, 0), (0, -1, 0), (0, 0, 1), (0, 0, -1), (1, 1, 0), (-1, -1, 0), (1, -1, 0), (-1, 1, 0), (1, 0, 1), (-1, 0, -1), (1, 0, -1), (-1, 0, 1), (0, 1, 1), (0, -1, -1), (0, 1, -1), (0, -1, 1))
OPPOSITE = (0, 2, 1, 4, 3, 6, 5, 8, 7, 10, 9, 12, 11, 14, 13, 16, 15, 18, 17)
RELAX_TIME = 0.8
STIFFNESS = 2.0
MARKER_AREA = 1.0
BOND_SPRING = 1.0
BOND_DAMPING = 0.5
HIGHEST = lax.Precision.HIGHEST


def lattice_weight(vector):
    return (1.0 / 3.0, 1.0 / 18.0, 1.0 / 36.0)[abs(vector[0]) + abs(vector[1]) + abs(vector[2])]


def cross_rows(first_rows, second_rows):
    return jnp.stack([first_rows[1] * second_rows[2] - first_rows[2] * second_rows[1],
                      first_rows[2] * second_rows[0] - first_rows[0] * second_rows[2],
                      first_rows[0] * second_rows[1] - first_rows[1] * second_rows[0]])


def project(vector, field):
    term_list = [vector[axis_number] * field[axis_number] for axis_number in range(3) if vector[axis_number] != 0]
    if not term_list:
        return jnp.zeros_like(field[0])
    return sum(term_list[1:], term_list[0])


def moments(populations):
    density = jnp.sum(populations, axis=0)
    velocity_table = jnp.array(LATTICE, jnp.float32)
    momentum = jnp.einsum("qd,qxyz->dxyz", velocity_table, populations, precision=HIGHEST)
    return density, momentum


def collide(populations, density, momentum, forcing):
    velocity = (momentum + 0.5 * forcing) / density
    speed_square = velocity[0] * velocity[0] + velocity[1] * velocity[1] + velocity[2] * velocity[2]
    flow_force = velocity[0] * forcing[0] + velocity[1] * forcing[1] + velocity[2] * forcing[2]
    factor = 1.0 - 0.5 / RELAX_TIME
    result = []
    for number, vector in enumerate(LATTICE):
        weight = lattice_weight(vector)
        along_flow = project(vector, velocity)
        along_force = project(vector, forcing)
        equilibrium = weight * density * (1.0 + 3.0 * along_flow + 4.5 * along_flow * along_flow - 1.5 * speed_square)
        source = factor * weight * (3.0 * (along_force - flow_force) + 9.0 * along_flow * along_force)
        current = populations[number]
        result.append(current - (current - equilibrium) / RELAX_TIME + source)
    return jnp.stack(result)


def wall_step(shifted, opposite, step_z):
    if step_z == 1:
        return jnp.concatenate([opposite[:, :, :1], shifted[:, :, :-1]], axis=2)
    if step_z == -1:
        return jnp.concatenate([shifted[:, :, 1:], opposite[:, :, -1:]], axis=2)
    return shifted


def stream(collided):
    result = []
    for number, vector in enumerate(LATTICE):
        shifted = jnp.roll(collided[number], (vector[0], vector[1]), axis=(0, 1))
        result.append(wall_step(shifted, collided[OPPOSITE[number]], vector[2]))
    return jnp.stack(result)


def reference(populations, grain_position, grain_motion, marker_grain, marker_offset, marker_weights, marker_cell, block_dest, bond_pairs, bond_rest):
    density, momentum = moments(populations)
    bare_velocity = momentum / density
    marker_total = marker_grain.shape[0]
    device = jnp.arange(marker_total, dtype=jnp.int32) // (BLK_DEV * MARKS)
    row_first = device // N_GY
    row_second = device % N_GY
    destination = jnp.repeat(block_dest, MARKS)
    owner_grain = row_first * GR_SLAB + marker_grain
    carried = grain_motion[:, owner_grain]
    surface = carried[:3] + cross_rows(carried[3:], marker_offset)
    local_x = marker_cell // (CY * CZ)
    local_y = (marker_cell // CZ) % CY
    local_z = marker_cell % CZ
    base_cell = ((destination * CX + local_x) * NY + row_second * CY + local_y) * NZ + local_z
    flat_velocity = bare_velocity.reshape(3, NX * NY * NZ)
    corner_cells = []
    for step_x in (0, 1):
        for step_y in (0, 1):
            for step_z in (0, 1):
                corner_cells.append((base_cell + (step_x * NY + step_y) * NZ + step_z).astype(jnp.int32))
    sampled = jnp.zeros_like(surface)
    for corner in range(8):
        sampled = sampled + marker_weights[corner] * flat_velocity[:, corner_cells[corner]]
    pushed = STIFFNESS * (surface - sampled)
    force_flat = jnp.zeros((3, NX * NY * NZ), jnp.float32)
    for corner in range(8):
        force_flat = force_flat.at[:, corner_cells[corner]].add(MARKER_AREA * marker_weights[corner] * pushed)
    forcing = force_flat.reshape(3, NX, NY, NZ)
    collided = collide(populations, density, momentum, forcing)
    populations_next = stream(collided)
    reaction = -MARKER_AREA * pushed
    marker_load = jnp.concatenate([reaction, cross_rows(marker_offset, reaction)], axis=0)
    hydro_load = jax.ops.segment_sum(marker_load.T, owner_grain, num_segments=GRAINS).T
    bond_total = bond_pairs.shape[1]
    bond_slab_index = jnp.arange(bond_total, dtype=jnp.int32) // BOND_SLAB
    first_end = bond_slab_index * GR_SLAB + bond_pairs[0]
    second_end = bond_slab_index * GR_SLAB + bond_pairs[1]
    stretch = grain_position[:, second_end] - grain_position[:, first_end]
    bond_force = BOND_SPRING * (stretch - bond_rest) + BOND_DAMPING * (grain_motion[:3, second_end] - grain_motion[:3, first_end])
    bond_torque = 0.5 * cross_rows(stretch, bond_force)
    bonded = jax.ops.segment_sum(jnp.concatenate([bond_force, bond_torque], axis=0).T, first_end, num_segments=GRAINS).T
    bonded = bonded + jax.ops.segment_sum(jnp.concatenate([-bond_force, bond_torque], axis=0).T, second_end, num_segments=GRAINS).T
    return populations_next, hydro_load + bonded
```

```python
import jax
import jax.numpy as jnp
from jax import lax
from jax.experimental import pallas as pl
from jax.experimental.pallas import tpu as pltpu
from jax.sharding import PartitionSpec as P

MARKS = 128
CAPB = 2
SLOT_ROWS = 24
BACK_ROWS = 8
EDGE_ROWS = 24
UNROLL = 8
REDUCE_STEPS = ((1, 2, 3), (4,))


LATTICE = (
    (0, 0, 0),
    (1, 0, 0),
    (-1, 0, 0),
    (0, 1, 0),
    (0, -1, 0),
    (0, 0, 1),
    (0, 0, -1),
    (1, 1, 0),
    (-1, -1, 0),
    (1, -1, 0),
    (-1, 1, 0),
    (1, 0, 1),
    (-1, 0, -1),
    (1, 0, -1),
    (-1, 0, 1),
    (0, 1, 1),
    (0, -1, -1),
    (0, 1, -1),
    (0, -1, 1),
)
OPPOSITE = (0, 2, 1, 4, 3, 6, 5, 8, 7, 10, 9, 12, 11, 14, 13, 16, 15, 18, 17)
RELAX_TIME = 0.8
STIFFNESS = 2.0
MARKER_AREA = 1.0
BOND_SPRING = 1.0
BOND_DAMPING = 0.5
UP_X = tuple(i for i, v in enumerate(LATTICE) if v[0] == 1)
DOWN_X = tuple(i for i, v in enumerate(LATTICE) if v[0] == -1)
UP_Y = tuple(i for i, v in enumerate(LATTICE) if v[1] == 1)
DOWN_Y = tuple(i for i, v in enumerate(LATTICE) if v[1] == -1)
NT = (((1,), (1,)), ((), ()))
NN = (((1,), (0,)), ((), ()))
VMEM = pl.BlockSpec(memory_space=pltpu.VMEM)
SMEM = pl.BlockSpec(memory_space=pltpu.SMEM)
HBM = pl.BlockSpec(memory_space=pltpu.HBM)
ANYWHERE = pl.BlockSpec(memory_space=pl.ANY)
F32 = jnp.float32
BF16 = jnp.bfloat16


def lattice_weight(vector):
    return (1.0 / 3.0, 1.0 / 18.0, 1.0 / 36.0)[abs(vector[0]) + abs(vector[1]) + abs(vector[2])]


def cross_rows(first_rows, second_rows):
    return [
        first_rows[1] * second_rows[2] - first_rows[2] * second_rows[1],
        first_rows[2] * second_rows[0] - first_rows[0] * second_rows[2],
        first_rows[0] * second_rows[1] - first_rows[1] * second_rows[0],
    ]


def rows_of(array):
    return [array[i : i + 1] for i in range(array.shape[0])]


def halves(value):
    high = value.astype(BF16)
    low = (value - high.astype(F32)).astype(BF16)
    return high, low


def thirds(value):
    high = value.astype(BF16)
    rest = value - high.astype(F32)
    middle = rest.astype(BF16)
    return high, middle, (rest - middle.astype(F32)).astype(BF16)


def one_hot(count, index_row):
    lanes = index_row.shape[1]
    grid = lax.broadcasted_iota(jnp.int32, (count, lanes), 0)
    return jnp.where(grid == index_row, 1.0, 0.0).astype(BF16)


def pick(state, table, dims):
    rows = state.shape[0]
    stacked = jnp.concatenate([t.astype(F32) for t in thirds(state)], axis=0).astype(BF16)
    got = lax.dot_general(stacked, table, dims, preferred_element_type=F32)
    return got[:rows] + got[rows : 2 * rows] + got[2 * rows :]


def pad_rows(value, rows):
    return jnp.concatenate([value, jnp.zeros((rows - value.shape[0], value.shape[1]), F32)], axis=0)


def fetch(sources, targets, sems):
    copies = [
        pltpu.make_async_copy(source, target, sems.at[index])
        for index, (source, target) in enumerate(zip(sources, targets))
    ]
    for copy in copies:
        copy.start()
    return copies


def pack_kernel(*refs):
    sources, (out, used, sems), held = refs[:6], refs[6:9], refs[9:]
    copies = fetch(sources, held, sems)
    dest, grain, cell, motion, offset, weights = held
    blocks = grain.shape[0]
    slab = motion.shape[1]
    out[...] = jnp.zeros_like(out)
    for brick in range(out.shape[0]):
        used[brick] = 0
    for copy in copies:
        copy.wait()
    state = pad_rows(motion[...], 8)
    half = lax.broadcasted_iota(jnp.int32, (8, MARKS), 0) // 4
    for block in range(blocks):
        span = slice(block * MARKS, (block + 1) * MARKS)
        carried = pick(state, one_hot(slab, grain[block : block + 1, :]), NN)
        moved = rows_of(carried)
        lever = rows_of(offset[:, span])
        turned = cross_rows(moved[3:6], lever)
        tail = [moved[i] + turned[i] for i in range(3)]
        tail.append(cell[block : block + 1, :].astype(F32))
        tail = jnp.concatenate(tail + tail, axis=0)
        brick = dest[block]
        slot = used[brick]
        used[brick] = slot + 1
        out[brick, pl.ds(pl.multiple_of(8 * slot, 8), 8), :] = weights[:, span]
        out[brick, 16:24, :] = jnp.where(half == slot, tail, out[brick, 16:24, :])


def bond_part(pairs, rest, position, motion, bonded):
    slab = position.shape[1]
    state = pad_rows(jnp.concatenate([position[...], motion[0:3, :]], axis=0), 8)
    first = one_hot(slab, pairs[0:1, :])
    second = one_hot(slab, pairs[1:2, :])
    near = pick(state, first, NN)
    far = pick(state, second, NN)
    stretch = far[:3] - near[:3]
    force = BOND_SPRING * (stretch - rest[...]) + BOND_DAMPING * (far[3:6] - near[3:6])
    torque = [0.5 * row for row in cross_rows(rows_of(stretch), rows_of(force))]
    torque = jnp.concatenate(torque, axis=0)
    blank = jnp.zeros((2, force.shape[1]), F32)
    total = pick(jnp.concatenate([force, torque, blank], axis=0), first, NT)
    total = total + pick(jnp.concatenate([-force, torque, blank], axis=0), second, NT)
    bonded[...] = total


def momentum_of(current):
    total = []
    for axis in range(3):
        value = None
        for number, vector in enumerate(LATTICE):
            if vector[axis] == 0:
                continue
            if value is None:
                value = current[number] if vector[axis] == 1 else -current[number]
            elif vector[axis] == 1:
                value = value + current[number]
            else:
                value = value - current[number]
        total.append(value)
    return total


def sum_of(values):
    values = list(values)
    while len(values) > 1:
        values = [
            values[i] + values[i + 1] if i + 1 < len(values) else values[i]
            for i in range(0, len(values), 2)
        ]
    return values[0]


def moment_kernel(populations, pairs, rest, position, motion, table, bonded):
    quantity, size_x, size_y, size_z = populations.shape
    planes = size_x * size_y
    for x in range(size_x):
        current = [populations[q, x] for q in range(quantity)]
        inverse = 1.0 / sum_of(current)
        for axis, value in enumerate(momentum_of(current)):
            speed = value * inverse
            for step in range(2):
                if step == 1:
                    speed = pltpu.roll(speed, size_z - 1, 1)
                high, low = halves(speed)
                first = (step * 3 + axis) * planes + x * size_y
                table[first : first + size_y, 0:size_z] = high
                table[first : first + size_y, size_z : 2 * size_z] = low
    bond_part(pairs, rest, position, motion, bonded)


def marker_tables(slots, size_x, size_y, size_z):
    cells = jnp.concatenate([slots[19:20], slots[23:24]], axis=1).astype(jnp.int32)
    weight = jnp.concatenate([slots[0:8], slots[8:16]], axis=1)
    place_x = lax.shift_right_logical(cells, (size_y * size_z).bit_length() - 1)
    place_y = lax.shift_right_logical(cells, size_z.bit_length() - 1) & (size_y - 1)
    place_z = cells & (size_z - 1)
    depth = one_hot(size_z, place_z)
    row = lax.broadcasted_iota(jnp.int32, (size_y, cells.shape[1]), 0)
    at_low = row == place_y
    at_high = row == place_y + 1
    shares = [[None] * size_x, [None] * size_x]
    for x in range(size_x):
        share = jnp.where(place_x == x - 1, weight[4:8], 0.0)
        share = jnp.where(place_x == x, weight[0:4], share)
        for step in range(2):
            value = jnp.where(at_high, share[2 + step : 3 + step], 0.0)
            shares[step][x] = jnp.where(at_low, share[step : step + 1], value)
    return depth, shares


def sample_kernel(slots, table, pushed, *, size):
    size_x, size_y, size_z = size
    planes = size_x * size_y

    def body(source, carry):
        rows = slots[source]
        depth, shares = marker_tables(rows, size_x, size_y, size_z)
        found = lax.dot_general(
            table[...],
            jnp.concatenate([depth, depth], axis=0),
            NN,
            preferred_element_type=F32,
        )
        target = jnp.concatenate([rows[16:19], rows[20:23]], axis=1)
        force = []
        for axis in range(3):
            value = None
            for step in range(2):
                for x in range(size_x):
                    first = (step * 3 + axis) * planes + x * size_y
                    term = shares[step][x] * found[first : first + size_y]
                    value = term if value is None else value + term
            sampled = jnp.sum(value, axis=0, keepdims=True)
            force.append(STIFFNESS * (target[axis : axis + 1] - sampled))
        blank = jnp.zeros_like(force[0])
        force = jnp.concatenate(force + [blank], axis=0)
        pushed[source] = jnp.concatenate([force[:, :MARKS], force[:, MARKS:]], axis=0)
        return carry

    lax.fori_loop(0, slots.shape[0], body, 0, unroll=UNROLL)


def spread_kernel(
    place, slots, pushed, populations, collided, near_x, far_x, near_y, far_y, total
):
    quantity, size_x, size_y, size_z = populations.shape
    planes = size_x * size_y
    total[...] = jnp.zeros_like(total)

    def body(source, carry):
        depth, shares = marker_tables(slots[source], size_x, size_y, size_z)
        both = pushed[source]
        force = jnp.concatenate([both[0:4], both[4:8]], axis=1)
        high = []
        low = []
        for step in range(2):
            for axis in range(3):
                for x in range(size_x):
                    one, two = halves(MARKER_AREA * force[axis : axis + 1] * shares[step][x])
                    high.append(one)
                    low.append(two)
        left = jnp.concatenate(
            [jnp.concatenate(high, axis=0), jnp.concatenate(low, axis=0)], axis=1
        )
        right = jnp.concatenate([depth, depth], axis=1)
        total[...] += lax.dot_general(left, right, NT, preferred_element_type=F32)
        return carry

    lax.fori_loop(0, slots.shape[0], body, 0, unroll=UNROLL)

    factor = 1.0 - 0.5 / RELAX_TIME
    for x in range(size_x):
        current = [populations[q, x] for q in range(quantity)]
        density = sum_of(current)
        inverse = 1.0 / density
        momentum = momentum_of(current)
        forcing = []
        for axis in range(3):
            first = axis * planes + x * size_y
            near = total[first : first + size_y]
            far = total[3 * planes + first : 3 * planes + first + size_y]
            forcing.append(near + pltpu.roll(far, 1, 1))
        velocity = [(momentum[a] + 0.5 * forcing[a]) * inverse for a in range(3)]
        speed_square = sum_of([v * v for v in velocity])
        flow_force = sum_of([velocity[a] * forcing[a] for a in range(3)])
        rest_flow = 1.0 - 1.5 * speed_square
        rest_force = -3.0 * flow_force
        for number, vector in enumerate(LATTICE):
            weight = lattice_weight(vector)
            flow = rest_flow
            push = rest_force
            if any(vector):
                along_flow = project(vector, velocity)
                along_force = project(vector, forcing)
                flow = flow + along_flow * (3.0 + 4.5 * along_flow)
                push = push + along_force * (3.0 + 9.0 * along_flow)
            value = (
                (1.0 - 1.0 / RELAX_TIME) * current[number]
                + (weight / RELAX_TIME) * density * flow
                + (factor * weight) * push
            )
            collided[number, x] = value
            if x == size_x - 1 and number in UP_X:
                put_face(place[0] == 0, near_x, far_x, UP_X.index(number), value)
            if x == 0 and number in DOWN_X:
                put_face(place[0] == 1, near_x, far_x, DOWN_X.index(number), value)
            if number in UP_Y:
                line = UP_Y.index(number) * size_x + x
                put_row(place[1] == 0, near_y, far_y, line, value[size_y - 1 : size_y])
            if number in DOWN_Y:
                line = DOWN_Y.index(number) * size_x + x
                put_row(place[1] == 1, near_y, far_y, line, value[0:1])
    filled = len(UP_Y) * size_x
    for face in (near_y, far_y):
        face[filled:] = jnp.zeros_like(face[filled:])


def put_face(to_near, near, far, index, value):
    @pl.when(to_near)
    def _():
        near[index] = value

    @pl.when(jnp.logical_not(to_near))
    def _():
        far[index] = value


def put_row(to_near, near, far, line, value):
    @pl.when(to_near)
    def _():
        near[line : line + 1] = value

    @pl.when(jnp.logical_not(to_near))
    def _():
        far[line : line + 1] = value


def edge_kernel(
    place, near_x, far_x, near_y, far_y, *refs, size_x
):
    parts, (near_out, far_out, total_out) = refs[:-3], refs[-3:]
    size_y = near_x.shape[1]
    filled = len(UP_Y) * size_x
    even_x = place[0] == 0
    from_x = lambda number, y: jnp.where(
        even_x, far_x[UP_X.index(number), y : y + 1], near_x[UP_X.index(number), y : y + 1]
    )
    to_x = lambda number, y: jnp.where(
        even_x, near_x[DOWN_X.index(number), y : y + 1], far_x[DOWN_X.index(number), y : y + 1]
    )
    top = size_y - 1
    up = jnp.concatenate([from_x(LATTICE.index((1, 1, 0)), top), to_x(LATTICE.index((-1, 1, 0)), top)], axis=0)
    down = jnp.concatenate([from_x(LATTICE.index((1, -1, 0)), 0), to_x(LATTICE.index((-1, -1, 0)), 0)], axis=0)
    even_y = place[1] == 0
    near_out[...] = near_y[...]
    far_out[...] = far_y[...]
    near_out[filled : filled + 2] = jnp.where(even_y, up, down)
    far_out[filled : filled + 2] = jnp.where(even_y, down, up)
    total_out[...] = sum_of([part[...] for part in parts])


def project(vector, field):
    value = None
    for axis in range(3):
        if vector[axis] == 0:
            continue
        if value is None:
            value = field[axis] if vector[axis] == 1 else -field[axis]
        elif vector[axis] == 1:
            value = value + field[axis]
        else:
            value = value - field[axis]
    return value


def stream_kernel(
    place, collided, near_x, far_x, near_y, far_y, *refs
):
    parts, (out, load, stage, sems) = refs[:-4], refs[-4:]
    quantity, size_x, size_y, size_z = collided.shape
    row = lax.broadcasted_iota(jnp.int32, (size_y, size_z), 0)
    lane = lax.broadcasted_iota(jnp.int32, (size_y, size_z), 1)
    even_x = place[0] == 0
    even_y = place[1] == 0
    filled = len(UP_Y) * size_x
    from_y = jnp.where(even_y, far_y[...], near_y[...])
    to_y = jnp.where(even_y, near_y[...], far_y[...])
    copies = []
    for x in (1, 2, 0, 3):
        for number, vector in enumerate(LATTICE):
            source = x - vector[0]
            inside = 0 <= source < size_x
            if inside:
                value = collided[number, source]
            elif vector[0] == 1:
                index = UP_X.index(number)
                value = jnp.where(even_x, far_x[index], near_x[index])
            else:
                index = DOWN_X.index(number)
                value = jnp.where(even_x, near_x[index], far_x[index])
            if vector[1]:
                face = from_y if vector[1] == 1 else to_y
                column = UP_Y if vector[1] == 1 else DOWN_Y
                if inside:
                    line = column.index(number) * size_x + source
                else:
                    line = filled if vector[0] == 1 else filled + 1
                ghost = face[line : line + 1]
                if vector[1] == 1:
                    value = jnp.where(row == 0, ghost, pltpu.roll(value, 1, 0))
                else:
                    value = jnp.where(row == size_y - 1, ghost, pltpu.roll(value, size_y - 1, 0))
            if vector[2]:
                back = collided[OPPOSITE[number], x]
                if vector[2] == 1:
                    value = jnp.where(lane == 0, back, pltpu.roll(value, 1, 1))
                else:
                    value = jnp.where(lane == size_z - 1, back, pltpu.roll(value, size_z - 1, 1))
            stage[number, x] = value
        copy = pltpu.make_async_copy(stage.at[:, x], out.at[:, x], sems.at[x])
        copy.start()
        copies.append(copy)
    total = sum_of([part[...] for part in parts])
    load[...] = total[: load.shape[0]]
    for copy in copies:
        copy.wait()


def grain_kernel(dest, grain, offset, returned, after, partial, used):
    blocks = grain.shape[0]
    slab = partial.shape[1]
    for brick in range(returned.shape[0]):
        used[brick] = 0
    total = None
    for block in range(blocks):
        span = slice(block * MARKS, (block + 1) * MARKS)
        brick = dest[block]
        slot = used[brick]
        used[brick] = slot + 1
        both = returned[brick]
        force = jnp.where(slot == 0, both[0:3], both[4:7])
        reaction = -MARKER_AREA * force
        torque = cross_rows(rows_of(offset[:, span]), rows_of(reaction))
        load = jnp.concatenate([reaction] + torque + [jnp.zeros((2, MARKS), F32)], axis=0)
        term = pick(load, one_hot(slab, grain[block : block + 1, :]), NT)
        total = term if total is None else total + term
    partial[...] = total


def cross(step):
    return [(i, i ^ step) for i in range(lax.axis_size("gy"))]


def swap(axis, step):
    count = lax.axis_size(axis)
    return [(i, (i + 1 if i % 2 == step else i - 1) % count) for i in range(count)]


def shards(
    populations,
    grain_position,
    grain_motion,
    marker_grain,
    marker_offset,
    marker_weights,
    marker_cell,
    block_dest,
    bond_pairs,
    bond_rest,
):
    quantity, size_x, size_y, size_z = populations.shape
    planes = size_x * size_y
    slab = grain_motion.shape[1]
    blocks = marker_grain.shape[0] // MARKS
    bricks = lax.axis_size("gx")
    shape = jax.ShapeDtypeStruct
    params = pltpu.CompilerParams(vmem_limit_bytes=48 * 1024 * 1024)
    grain_blocks = marker_grain.reshape(blocks, MARKS)
    cell_blocks = marker_cell.reshape(blocks, MARKS)

    place = jnp.stack([lax.axis_index("gx") & 1, lax.axis_index("gy") & 1]).astype(jnp.int32)
    outgoing = pl.pallas_call(
        pack_kernel,
        out_shape=shape((bricks, SLOT_ROWS, MARKS), F32),
        in_specs=[HBM] * 6,
        out_specs=VMEM,
        scratch_shapes=[
            pltpu.SMEM((bricks,), jnp.int32),
            pltpu.SemaphoreType.DMA((6,)),
            pltpu.SMEM(block_dest.shape, jnp.int32),
            pltpu.VMEM(grain_blocks.shape, jnp.int32),
            pltpu.VMEM(cell_blocks.shape, jnp.int32),
            pltpu.VMEM(grain_motion.shape, F32),
            pltpu.VMEM(marker_offset.shape, F32),
            pltpu.VMEM(marker_weights.shape, F32),
        ],
        compiler_params=params,
        name="pack",
    )(
        *[
            pltpu.with_memory_space_constraint(array, pltpu.HBM)
            for array in (
                block_dest,
                grain_blocks,
                cell_blocks,
                grain_motion,
                marker_offset,
                marker_weights,
            )
        ]
    )
    slots = lax.all_to_all(outgoing, "gx", split_axis=0, concat_axis=0, tiled=True)

    table, bonded = pl.pallas_call(
        moment_kernel,
        out_shape=[shape((6 * planes, 2 * size_z), BF16), shape((8, slab), F32)],
        in_specs=[VMEM] * 5,
        out_specs=[VMEM] * 2,
        compiler_params=params,
        cost_estimate=pl.CostEstimate(flops=20000000, bytes_accessed=4000000, transcendentals=0),
        name="moments",
    )(populations, bond_pairs, bond_rest, grain_position, grain_motion)

    pushed = pl.pallas_call(
        lambda *refs: sample_kernel(*refs, size=(size_x, size_y, size_z)),
        out_shape=shape((bricks, BACK_ROWS, MARKS), F32),
        in_specs=[VMEM] * 2,
        out_specs=VMEM,
        compiler_params=params,
        name="sample",
    )(slots, table)
    returned = lax.all_to_all(pushed, "gx", split_axis=0, concat_axis=0, tiled=True)

    collided, *faces = pl.pallas_call(
        spread_kernel,
        out_shape=[
            shape(populations.shape, F32),
            shape((len(UP_X), size_y, size_z), F32),
            shape((len(UP_X), size_y, size_z), F32),
            shape((EDGE_ROWS, size_z), F32),
            shape((EDGE_ROWS, size_z), F32),
        ],
        in_specs=[SMEM] + [VMEM] * 3,
        out_specs=[VMEM] * 5,
        scratch_shapes=[pltpu.VMEM((6 * planes, size_z), F32)],
        compiler_params=params,
        cost_estimate=pl.CostEstimate(
            flops=6000000000, bytes_accessed=8000000, transcendentals=0
        ),
        name="spread",
    )(place, slots, pushed, populations)

    near_x = lax.ppermute(faces[0], "gx", swap("gx", 0))
    far_x = lax.ppermute(faces[1], "gx", swap("gx", 1))

    partial = pl.pallas_call(
        grain_kernel,
        out_shape=shape((8, slab), F32),
        in_specs=[SMEM] + [VMEM] * 3 + [ANYWHERE],
        out_specs=VMEM,
        scratch_shapes=[pltpu.SMEM((bricks,), jnp.int32)],
        compiler_params=params,
        name="grain",
    )(block_dest, grain_blocks, marker_offset, returned, faces[2])
    first, second = REDUCE_STEPS
    parts = [partial] + [lax.ppermute(partial, "gy", cross(step)) for step in first]

    near_y, far_y, total = pl.pallas_call(
        lambda *refs: edge_kernel(*refs, size_x=size_x),
        out_shape=[shape((EDGE_ROWS, size_z), F32)] * 2 + [shape((8, slab), F32)],
        in_specs=[SMEM] + [VMEM] * (4 + len(parts)),
        out_specs=[VMEM] * 3,
        compiler_params=params,
        name="edge",
    )(place, near_x, far_x, faces[2], faces[3], *parts)
    near_y = lax.ppermute(near_y, "gy", swap("gy", 0))
    far_y = lax.ppermute(far_y, "gy", swap("gy", 1))
    parts = [bonded, total] + [lax.ppermute(total, "gy", cross(step)) for step in second]

    populations_next, grain_load = pl.pallas_call(
        stream_kernel,
        out_shape=[shape(populations.shape, F32), shape((6, slab), F32)],
        in_specs=[SMEM] + [VMEM] * (5 + len(parts)),
        out_specs=[ANYWHERE, VMEM],
        scratch_shapes=[
            pltpu.VMEM(populations.shape, F32),
            pltpu.SemaphoreType.DMA((size_x,)),
        ],
        compiler_params=params,
        name="stream",
    )(place, collided, near_x, far_x, near_y, far_y, *parts)
    return populations_next, grain_load


def solution(mesh):
    in_specs = (
        P(None, "gx", "gy", None),
        P(None, "gx"),
        P(None, "gx"),
        P(("gx", "gy")),
        P(None, ("gx", "gy")),
        P(None, ("gx", "gy")),
        P(("gx", "gy")),
        P(("gx", "gy")),
        P(None, "gx"),
        P(None, "gx"),
    )
    out_specs = (P(None, "gx", "gy", None), P(None, "gx"))
    return jax.shard_map(shards, mesh=mesh, in_specs=in_specs, out_specs=out_specs, check_vma=False)
```

```python
import jax
import jax.numpy as jnp
from jax import lax
from jax.experimental import pallas as pl
from jax.experimental.pallas import tpu as pltpu
from jax.sharding import PartitionSpec as P

MARKS = 128
CAPB = 2
SLOT_ROWS = 24
BACK_ROWS = 8
EDGE_ROWS = 24
SAMPLE_GROUP = 2
SAMPLE_UNROLL = 16
SPREAD_GROUP = 8
SPREAD_UNROLL = 4
CHUNK = 8


LATTICE = (
    (0, 0, 0),
    (1, 0, 0),
    (-1, 0, 0),
    (0, 1, 0),
    (0, -1, 0),
    (0, 0, 1),
    (0, 0, -1),
    (1, 1, 0),
    (-1, -1, 0),
    (1, -1, 0),
    (-1, 1, 0),
    (1, 0, 1),
    (-1, 0, -1),
    (1, 0, -1),
    (-1, 0, 1),
    (0, 1, 1),
    (0, -1, -1),
    (0, 1, -1),
    (0, -1, 1),
)
OPPOSITE = (0, 2, 1, 4, 3, 6, 5, 8, 7, 10, 9, 12, 11, 14, 13, 16, 15, 18, 17)
RELAX_TIME = 0.8
STIFFNESS = 2.0
MARKER_AREA = 1.0
BOND_SPRING = 1.0
BOND_DAMPING = 0.5
UP_X = tuple(i for i, v in enumerate(LATTICE) if v[0] == 1)
DOWN_X = tuple(i for i, v in enumerate(LATTICE) if v[0] == -1)
UP_Y = tuple(i for i, v in enumerate(LATTICE) if v[1] == 1)
DOWN_Y = tuple(i for i, v in enumerate(LATTICE) if v[1] == -1)
NT = (((1,), (1,)), ((), ()))
NN = (((1,), (0,)), ((), ()))
VMEM = pl.BlockSpec(memory_space=pltpu.VMEM)
SMEM = pl.BlockSpec(memory_space=pltpu.SMEM)
HBM = pl.BlockSpec(memory_space=pltpu.HBM)
F32 = jnp.float32
BF16 = jnp.bfloat16


def lattice_weight(vector):
    return (1.0 / 3.0, 1.0 / 18.0, 1.0 / 36.0)[abs(vector[0]) + abs(vector[1]) + abs(vector[2])]


def cross_rows(first_rows, second_rows):
    return [
        first_rows[1] * second_rows[2] - first_rows[2] * second_rows[1],
        first_rows[2] * second_rows[0] - first_rows[0] * second_rows[2],
        first_rows[0] * second_rows[1] - first_rows[1] * second_rows[0],
    ]


def rows_of(array):
    return [array[i : i + 1] for i in range(array.shape[0])]


def halves(value):
    high = value.astype(BF16)
    low = (value - high.astype(F32)).astype(BF16)
    return high, low


def thirds(value):
    high = value.astype(BF16)
    rest = value - high.astype(F32)
    middle = rest.astype(BF16)
    return high, middle, (rest - middle.astype(F32)).astype(BF16)


def one_hot(count, index_row):
    lanes = index_row.shape[1]
    grid = lax.broadcasted_iota(jnp.int32, (count, lanes), 0)
    return jnp.where(grid == index_row, 1.0, 0.0).astype(BF16)


def pick(state, table, dims):
    rows = state.shape[0]
    stacked = jnp.concatenate([t.astype(F32) for t in thirds(state)], axis=0).astype(BF16)
    got = lax.dot_general(stacked, table, dims, preferred_element_type=F32)
    return got[:rows] + got[rows : 2 * rows] + got[2 * rows :]


def pad_rows(value, rows):
    return jnp.concatenate([value, jnp.zeros((rows - value.shape[0], value.shape[1]), F32)], axis=0)


def fetch(sources, targets, sems):
    copies = [
        pltpu.make_async_copy(source, target, sems.at[index])
        for index, (source, target) in enumerate(zip(sources, targets))
    ]
    for copy in copies:
        copy.start()
    return copies


def pack_kernel(*refs):
    sources, (out, used, sems), held = refs[:6], refs[6:9], refs[9:]
    copies = fetch(sources, held, sems)
    dest, grain, cell, motion, offset, weights = held
    blocks = grain.shape[0]
    slab = motion.shape[1]
    out[...] = jnp.zeros_like(out)
    for brick in range(out.shape[0]):
        used[brick] = 0
    for copy in copies:
        copy.wait()
    state = pad_rows(motion[...], 8)
    half = lax.broadcasted_iota(jnp.int32, (8, MARKS), 0) // 4
    for block in range(blocks):
        span = slice(block * MARKS, (block + 1) * MARKS)
        carried = pick(state, one_hot(slab, grain[block : block + 1, :]), NN)
        moved = rows_of(carried)
        lever = rows_of(offset[:, span])
        turned = cross_rows(moved[3:6], lever)
        tail = [moved[i] + turned[i] for i in range(3)]
        tail.append(cell[block : block + 1, :].astype(F32))
        tail = jnp.concatenate(tail + tail, axis=0)
        brick = dest[block]
        slot = used[brick]
        used[brick] = slot + 1
        out[brick, pl.ds(pl.multiple_of(8 * slot, 8), 8), :] = weights[:, span]
        out[brick, 16:24, :] = jnp.where(half == slot, tail, out[brick, 16:24, :])


def bond_part(pairs, rest, position, motion, bonded):
    slab = position.shape[1]
    state = pad_rows(jnp.concatenate([position[...], motion[0:3, :]], axis=0), 8)
    first = one_hot(slab, pairs[0:1, :])
    second = one_hot(slab, pairs[1:2, :])
    near = pick(state, first, NN)
    far = pick(state, second, NN)
    stretch = far[:3] - near[:3]
    force = BOND_SPRING * (stretch - rest[...]) + BOND_DAMPING * (far[3:6] - near[3:6])
    torque = [0.5 * row for row in cross_rows(rows_of(stretch), rows_of(force))]
    torque = jnp.concatenate(torque, axis=0)
    blank = jnp.zeros((2, force.shape[1]), F32)
    total = pick(jnp.concatenate([force, torque, blank], axis=0), first, NT)
    total = total + pick(jnp.concatenate([-force, torque, blank], axis=0), second, NT)
    bonded[...] = total


def momentum_of(current):
    total = []
    for axis in range(3):
        value = None
        for number, vector in enumerate(LATTICE):
            if vector[axis] == 0:
                continue
            if value is None:
                value = current[number] if vector[axis] == 1 else -current[number]
            elif vector[axis] == 1:
                value = value + current[number]
            else:
                value = value - current[number]
        total.append(value)
    return total


def sum_of(values):
    values = list(values)
    while len(values) > 1:
        values = [
            values[i] + values[i + 1] if i + 1 < len(values) else values[i]
            for i in range(0, len(values), 2)
        ]
    return values[0]


def moment_kernel(populations, pairs, rest, position, motion, table, bonded):
    quantity, size_x, size_y, size_z = populations.shape
    planes = size_x * size_y
    for x in range(size_x):
        current = [populations[q, x] for q in range(quantity)]
        inverse = 1.0 / sum_of(current)
        for axis, value in enumerate(momentum_of(current)):
            speed = value * inverse
            for step in range(2):
                if step == 1:
                    speed = pltpu.roll(speed, size_z - 1, 1)
                high, low = halves(speed)
                first = (step * 3 + axis) * planes + x * size_y
                table[first : first + size_y, 0:size_z] = high
                table[first : first + size_y, size_z : 2 * size_z] = low
    bond_part(pairs, rest, position, motion, bonded)


def marker_places(slots, size_x, size_y, size_z):
    cells = jnp.concatenate([slots[19:20], slots[23:24]], axis=1).astype(jnp.int32)
    weight = jnp.concatenate([slots[0:8], slots[8:16]], axis=1)
    place_x = lax.shift_right_logical(cells, (size_y * size_z).bit_length() - 1)
    place_y = lax.shift_right_logical(cells, size_z.bit_length() - 1) & (size_y - 1)
    place_z = cells & (size_z - 1)
    shares = []
    for x in range(size_x):
        share = jnp.where(place_x == x - 1, weight[4:8], 0.0)
        shares.append(jnp.where(place_x == x, weight[0:4], share))
    return shares, place_y, one_hot(size_z, place_z)


def marker_shares(shares, place_y, size_y):
    row = lax.broadcasted_iota(jnp.int32, (size_y, place_y.shape[1]), 0)
    at_low = row == place_y
    at_high = row == place_y + 1
    tables = [[], []]
    for share in shares:
        for corner in range(2):
            value = jnp.where(at_high, share[2 + corner : 3 + corner], 0.0)
            tables[corner].append(jnp.where(at_low, share[corner : corner + 1], value))
    return tables


def marker_halves(shares, place_y, size_y):
    at_low = one_hot(size_y, place_y)
    at_high = one_hot(size_y, place_y + 1)
    tables = [[], []]
    for part in range(2):
        split = [halves(share)[part] for share in shares]
        for corner in range(2):
            for share in split:
                low = at_low * share[corner : corner + 1]
                high = at_high * share[2 + corner : 3 + corner]
                tables[part].append(low + high)
    return [jnp.concatenate(table, axis=0) for table in tables]


def sample_kernel(slots, table, pushed, *, size):
    size_x, size_y, size_z = size
    planes = size_x * size_y

    def body(step, carry):
        tables = []
        for part in range(SAMPLE_GROUP):
            rows = slots[step * SAMPLE_GROUP + part]
            shares, place_y, depth = marker_places(rows, size_x, size_y, size_z)
            tables.append((rows, depth, marker_shares(shares, place_y, size_y)))
        depth = jnp.concatenate([entry[1] for entry in tables], axis=1)
        depth = jnp.concatenate([depth, depth], axis=0)
        found = lax.dot_general(table[...], depth, NN, preferred_element_type=F32)
        for part, (rows, _, shares) in enumerate(tables):
            span = slice(part * 2 * MARKS, (part + 1) * 2 * MARKS)
            target = jnp.concatenate([rows[16:19], rows[20:23]], axis=1)
            force = []
            for axis in range(3):
                value = None
                for corner in range(2):
                    for x in range(size_x):
                        first = (corner * 3 + axis) * planes + x * size_y
                        term = shares[corner][x] * found[first : first + size_y, span]
                        value = term if value is None else value + term
                sampled = jnp.sum(value, axis=0, keepdims=True)
                force.append(STIFFNESS * (target[axis : axis + 1] - sampled))
            blank = jnp.zeros_like(force[0])
            force = jnp.concatenate(force + [blank], axis=0)
            pushed[step * SAMPLE_GROUP + part] = jnp.concatenate(
                [force[:, :MARKS], force[:, MARKS:]], axis=0
            )
        return carry

    lax.fori_loop(0, slots.shape[0] // SAMPLE_GROUP, body, 0, unroll=SAMPLE_UNROLL)


def spread_kernel(
    place, slots, pushed, populations, collided, near_x, far_x, near_y, far_y, total
):
    quantity, size_x, size_y, size_z = populations.shape
    planes = size_x * size_y
    total[...] = jnp.zeros_like(total)

    def body(step, carry):
        wide, thin, strong, weak = [], [], [], []
        for part in range(SPREAD_GROUP):
            source = step * SPREAD_GROUP + part
            shares, place_y, depth = marker_places(slots[source], size_x, size_y, size_z)
            first, second = marker_halves(shares, place_y, size_y)
            both = pushed[source]
            force = MARKER_AREA * jnp.concatenate([both[0:4], both[4:8]], axis=1)
            high, low = halves(force)
            wide.append(first)
            thin.append(second)
            strong.append(jnp.concatenate([depth * high[a : a + 1] for a in range(3)], axis=0))
            weak.append(jnp.concatenate([depth * low[a : a + 1] for a in range(3)], axis=0))
        wide, thin, strong, weak = (
            jnp.concatenate(part, axis=1) for part in (wide, thin, strong, weak)
        )
        most = lax.dot_general(
            jnp.concatenate([strong, weak], axis=0), wide, NT, preferred_element_type=F32
        )
        rest = lax.dot_general(strong, thin, NT, preferred_element_type=F32)
        height = strong.shape[0]
        total[...] += most[:height] + (most[height:] + rest)
        return carry

    lax.fori_loop(0, slots.shape[0] // SPREAD_GROUP, body, 0, unroll=SPREAD_UNROLL)

    for axis in range(3):
        span = slice(axis * size_z, (axis + 1) * size_z)
        both = total[span, :planes] + pltpu.roll(total[span, planes:], 1, 0)
        total[span, :planes] = both.T

    factor = 1.0 - 0.5 / RELAX_TIME
    for x in range(size_x):
        for y in range(0, size_y, CHUNK):
            rows = slice(y, y + CHUNK)
            current = [populations[q, x, rows] for q in range(quantity)]
            density = sum_of(current)
            inverse = 1.0 / density
            momentum = momentum_of(current)
            forcing = []
            for axis in range(3):
                first = axis * size_z + x * size_y + y
                forcing.append(total[first : first + CHUNK, :size_z])
            velocity = [(momentum[a] + 0.5 * forcing[a]) * inverse for a in range(3)]
            speed_square = sum_of([v * v for v in velocity])
            flow_force = sum_of([velocity[a] * forcing[a] for a in range(3)])
            rest_flow = 1.0 - 1.5 * speed_square
            rest_force = -3.0 * flow_force
            for number, vector in enumerate(LATTICE):
                weight = lattice_weight(vector)
                flow = rest_flow
                push = rest_force
                if any(vector):
                    along_flow = project(vector, velocity)
                    along_force = project(vector, forcing)
                    flow = flow + along_flow * (3.0 + 4.5 * along_flow)
                    push = push + along_force * (3.0 + 9.0 * along_flow)
                collided[number, x, rows] = (
                    (1.0 - 1.0 / RELAX_TIME) * current[number]
                    + (weight / RELAX_TIME) * density * flow
                    + (factor * weight) * push
                )

    even_x = place[0] == 0
    for index, (up, down) in enumerate(zip(UP_X, DOWN_X)):
        top = collided[up, size_x - 1]
        bottom = collided[down, 0]
        near_x[index] = jnp.where(even_x, top, bottom)
        far_x[index] = jnp.where(even_x, bottom, top)
    even_y = place[1] == 0
    for index, (up, down) in enumerate(zip(UP_Y, DOWN_Y)):
        for x in range(size_x):
            top = collided[up, x, size_y - 1 : size_y]
            bottom = collided[down, x, 0:1]
            line = index * size_x + x
            near_y[line : line + 1] = jnp.where(even_y, top, bottom)
            far_y[line : line + 1] = jnp.where(even_y, bottom, top)
    filled = len(UP_Y) * size_x
    for face in (near_y, far_y):
        face[filled:] = jnp.zeros_like(face[filled:])


def edge_kernel(
    place, near_x, far_x, near_y, far_y, partial, near_out, far_out, *, size_x
):
    size_y = near_x.shape[1]
    filled = len(UP_Y) * size_x
    even_x = place[0] == 0
    from_x = lambda number, y: jnp.where(
        even_x, far_x[UP_X.index(number), y : y + 1], near_x[UP_X.index(number), y : y + 1]
    )
    to_x = lambda number, y: jnp.where(
        even_x, near_x[DOWN_X.index(number), y : y + 1], far_x[DOWN_X.index(number), y : y + 1]
    )
    top = size_y - 1
    up = jnp.concatenate([from_x(LATTICE.index((1, 1, 0)), top), to_x(LATTICE.index((-1, 1, 0)), top)], axis=0)
    down = jnp.concatenate([from_x(LATTICE.index((1, -1, 0)), 0), to_x(LATTICE.index((-1, -1, 0)), 0)], axis=0)
    even_y = place[1] == 0
    near_out[:EDGE_ROWS] = near_y[...]
    far_out[...] = far_y[...]
    width = near_out.shape[1]
    for part in range(partial.shape[1] // width):
        first = EDGE_ROWS + 8 * part
        near_out[first : first + 8] = partial[:, part * width : (part + 1) * width]
    near_out[filled : filled + 2] = jnp.where(even_y, up, down)
    far_out[filled : filled + 2] = jnp.where(even_y, down, up)


def pair_kernel(partial, near_y, total):
    width = near_y.shape[1]
    for part in range(partial.shape[1] // width):
        first = EDGE_ROWS + 8 * part
        span = slice(part * width, (part + 1) * width)
        total[:, span] = partial[:, span] + near_y[first : first + 8]


def project(vector, field):
    value = None
    for axis in range(3):
        if vector[axis] == 0:
            continue
        if value is None:
            value = field[axis] if vector[axis] == 1 else -field[axis]
        elif vector[axis] == 1:
            value = value + field[axis]
        else:
            value = value - field[axis]
    return value


def stream_kernel(place, collided, near_x, far_x, out, strips, stage, sems):
    quantity, size_x, size_y, size_z = collided.shape
    lane = lax.broadcasted_iota(jnp.int32, (size_y, size_z), 1)
    even_x = place[0] == 0
    copies = []
    for x in (1, 2, 0, 3):
        for number, vector in enumerate(LATTICE):
            source = x - vector[0]
            if 0 <= source < size_x:
                value = collided[number, source]
            elif vector[0] == 1:
                index = UP_X.index(number)
                value = jnp.where(even_x, far_x[index], near_x[index])
            else:
                index = DOWN_X.index(number)
                value = jnp.where(even_x, near_x[index], far_x[index])
            if vector[1]:
                value = pltpu.roll(value, 1 if vector[1] == 1 else size_y - 1, 0)
            if vector[2]:
                back = collided[OPPOSITE[number], x]
                if vector[2] == 1:
                    value = jnp.where(lane == 0, back, pltpu.roll(value, 1, 1))
                else:
                    value = jnp.where(lane == size_z - 1, back, pltpu.roll(value, size_z - 1, 1))
            stage[number, x] = value
            if vector[1] == 1:
                strips[UP_Y.index(number), x] = value[:8]
            elif vector[1] == -1:
                strips[len(UP_Y) + DOWN_Y.index(number), x] = value[size_y - 8 :]
        copy = pltpu.make_async_copy(stage.at[:, x], out.at[:, x], sems.at[x])
        copy.start()
        copies.append(copy)
    for copy in copies:
        copy.wait()


def rim_kernel(place, strips, near_y, far_y, *refs):
    parts, (given, out, load, stage, sems) = refs[:-5], refs[-5:]
    size_x, size_y, size_z = out.shape[1:]
    row = lax.broadcasted_iota(jnp.int32, (8, size_z), 0)
    lane = lax.broadcasted_iota(jnp.int32, (8, size_z), 1)
    even_y = place[1] == 0
    filled = len(UP_Y) * size_x
    near, far = near_y[:EDGE_ROWS], far_y[...]
    from_y = jnp.where(even_y, far, near)
    to_y = jnp.where(even_y, near, far)
    copies = []
    for group, (face, column, edge) in enumerate(((from_y, UP_Y, 0), (to_y, DOWN_Y, 7))):
        for index, number in enumerate(column):
            vector = LATTICE[number]
            slot = group * len(UP_Y) + index
            for x in range(size_x):
                source = x - vector[0]
                if 0 <= source < size_x:
                    line = index * size_x + source
                else:
                    line = filled if vector[0] == 1 else filled + 1
                ghost = jnp.broadcast_to(face[line : line + 1], (8, size_z))
                replace = row == edge
                if vector[2] == 1:
                    ghost = pltpu.roll(ghost, 1, 1)
                    replace = jnp.logical_and(replace, lane != 0)
                elif vector[2] == -1:
                    ghost = pltpu.roll(ghost, size_z - 1, 1)
                    replace = jnp.logical_and(replace, lane != size_z - 1)
                stage[slot, x] = jnp.where(replace, ghost, strips[slot, x])
            rows = pl.ds(0 if edge == 0 else size_y - 8, 8)
            copy = pltpu.make_async_copy(stage.at[slot], out.at[number, :, rows], sems.at[slot])
            copy.start()
            copies.append(copy)
    total = sum_of([part[...] for part in parts])
    load[...] = total[: load.shape[0]]
    for copy in copies:
        copy.wait()


def grain_kernel(dest, grain, offset, returned, after, partial, used):
    blocks = grain.shape[0]
    slab = partial.shape[1]
    for brick in range(returned.shape[0]):
        used[brick] = 0
    total = None
    for block in range(blocks):
        span = slice(block * MARKS, (block + 1) * MARKS)
        brick = dest[block]
        slot = used[brick]
        used[brick] = slot + 1
        both = returned[brick]
        force = jnp.where(slot == 0, both[0:3], both[4:7])
        reaction = -MARKER_AREA * force
        torque = cross_rows(rows_of(offset[:, span]), rows_of(reaction))
        load = jnp.concatenate([reaction] + torque + [jnp.zeros((2, MARKS), F32)], axis=0)
        term = pick(load, one_hot(slab, grain[block : block + 1, :]), NT)
        total = term if total is None else total + term
    partial[...] = total


def cross(step):
    return [(i, i ^ step) for i in range(lax.axis_size("gy"))]


def swap(axis, step):
    count = lax.axis_size(axis)
    return [(i, (i + 1 if i % 2 == step else i - 1) % count) for i in range(count)]


def shards(
    populations,
    grain_position,
    grain_motion,
    marker_grain,
    marker_offset,
    marker_weights,
    marker_cell,
    block_dest,
    bond_pairs,
    bond_rest,
):
    quantity, size_x, size_y, size_z = populations.shape
    planes = size_x * size_y
    slab = grain_motion.shape[1]
    blocks = marker_grain.shape[0] // MARKS
    bricks = lax.axis_size("gx")
    shape = jax.ShapeDtypeStruct
    params = pltpu.CompilerParams(vmem_limit_bytes=48 * 1024 * 1024)
    grain_blocks = marker_grain.reshape(blocks, MARKS)
    cell_blocks = marker_cell.reshape(blocks, MARKS)

    place = jnp.stack([lax.axis_index("gx") & 1, lax.axis_index("gy") & 1]).astype(jnp.int32)
    outgoing = pl.pallas_call(
        pack_kernel,
        out_shape=shape((bricks, SLOT_ROWS, MARKS), F32),
        in_specs=[HBM] * 6,
        out_specs=VMEM,
        scratch_shapes=[
            pltpu.SMEM((bricks,), jnp.int32),
            pltpu.SemaphoreType.DMA((6,)),
            pltpu.SMEM(block_dest.shape, jnp.int32),
            pltpu.VMEM(grain_blocks.shape, jnp.int32),
            pltpu.VMEM(cell_blocks.shape, jnp.int32),
            pltpu.VMEM(grain_motion.shape, F32),
            pltpu.VMEM(marker_offset.shape, F32),
            pltpu.VMEM(marker_weights.shape, F32),
        ],
        compiler_params=params,
        name="pack",
    )(
        *[
            pltpu.with_memory_space_constraint(array, pltpu.HBM)
            for array in (
                block_dest,
                grain_blocks,
                cell_blocks,
                grain_motion,
                marker_offset,
                marker_weights,
            )
        ]
    )
    slots = lax.all_to_all(outgoing, "gx", split_axis=0, concat_axis=0, tiled=True)

    table, bonded = pl.pallas_call(
        moment_kernel,
        out_shape=[shape((6 * planes, 2 * size_z), BF16), shape((8, slab), F32)],
        in_specs=[VMEM] * 5,
        out_specs=[VMEM] * 2,
        compiler_params=params,
        cost_estimate=pl.CostEstimate(flops=20000000, bytes_accessed=4000000, transcendentals=0),
        name="moments",
    )(populations, bond_pairs, bond_rest, grain_position, grain_motion)

    pushed = pl.pallas_call(
        lambda *refs: sample_kernel(*refs, size=(size_x, size_y, size_z)),
        out_shape=shape((bricks, BACK_ROWS, MARKS), F32),
        in_specs=[VMEM] * 2,
        out_specs=VMEM,
        compiler_params=params,
        name="sample",
    )(slots, table)
    returned = lax.all_to_all(pushed, "gx", split_axis=0, concat_axis=0, tiled=True)

    collided, *faces = pl.pallas_call(
        spread_kernel,
        out_shape=[
            shape(populations.shape, F32),
            shape((len(UP_X), size_y, size_z), F32),
            shape((len(UP_X), size_y, size_z), F32),
            shape((EDGE_ROWS, size_z), F32),
            shape((EDGE_ROWS, size_z), F32),
        ],
        in_specs=[SMEM] + [VMEM] * 3,
        out_specs=[VMEM] * 5,
        scratch_shapes=[pltpu.VMEM((3 * size_z, 2 * planes), F32)],
        compiler_params=params,
        cost_estimate=pl.CostEstimate(
            flops=6000000000, bytes_accessed=8000000, transcendentals=0
        ),
        name="spread",
    )(place, slots, pushed, populations)

    partial = pl.pallas_call(
        grain_kernel,
        out_shape=shape((8, slab), F32),
        in_specs=[SMEM] + [VMEM] * 3 + [HBM],
        out_specs=VMEM,
        scratch_shapes=[pltpu.SMEM((bricks,), jnp.int32)],
        compiler_params=params,
        name="grain",
    )(block_dest, grain_blocks, marker_offset, returned, faces[2])
    near_x = lax.ppermute(faces[0], "gx", swap("gx", 0))
    far_x = lax.ppermute(faces[1], "gx", swap("gx", 1))
    near_y, far_y = pl.pallas_call(
        lambda *refs: edge_kernel(*refs, size_x=size_x),
        out_shape=[
            shape((EDGE_ROWS + 8 * slab // size_z, size_z), F32),
            shape((EDGE_ROWS, size_z), F32),
        ],
        in_specs=[SMEM] + [VMEM] * 5,
        out_specs=[VMEM] * 2,
        compiler_params=params,
        name="edge",
    )(place, near_x, far_x, faces[2], faces[3], partial)
    near_y = lax.ppermute(near_y, "gy", swap("gy", 0))
    far_y = lax.ppermute(far_y, "gy", swap("gy", 1))
    total = pl.pallas_call(
        pair_kernel,
        out_shape=shape((8, slab), F32),
        in_specs=[VMEM] * 2,
        out_specs=VMEM,
        compiler_params=params,
        name="pair",
    )(partial, near_y)
    parts = [bonded, total]
    parts += [lax.ppermute(total, "gy", cross(step)) for step in range(2, lax.axis_size("gy"), 2)]

    streamed, strips = pl.pallas_call(
        stream_kernel,
        out_shape=[
            shape(populations.shape, F32),
            shape((len(UP_Y) + len(DOWN_Y), size_x, 8, size_z), F32),
        ],
        in_specs=[SMEM] + [VMEM] * 3,
        out_specs=[HBM, VMEM],
        scratch_shapes=[
            pltpu.VMEM(populations.shape, F32),
            pltpu.SemaphoreType.DMA((size_x,)),
        ],
        compiler_params=params,
        cost_estimate=pl.CostEstimate(flops=20000000, bytes_accessed=4000000, transcendentals=0),
        name="stream",
    )(place, collided, near_x, far_x)

    populations_next, grain_load = pl.pallas_call(
        rim_kernel,
        out_shape=[shape(populations.shape, F32), shape((6, slab), F32)],
        in_specs=[SMEM] + [VMEM] * (3 + len(parts)) + [HBM],
        out_specs=[HBM, VMEM],
        scratch_shapes=[
            pltpu.VMEM(strips.shape, F32),
            pltpu.SemaphoreType.DMA((strips.shape[0],)),
        ],
        input_output_aliases={4 + len(parts): 0},
        compiler_params=params,
        name="rim",
    )(place, strips, near_y, far_y, *parts, streamed)
    return populations_next, grain_load


def solution(mesh):
    in_specs = (
        P(None, "gx", "gy", None),
        P(None, "gx"),
        P(None, "gx"),
        P(("gx", "gy")),
        P(None, ("gx", "gy")),
        P(None, ("gx", "gy")),
        P(("gx", "gy")),
        P(("gx", "gy")),
        P(None, "gx"),
        P(None, "gx"),
    )
    out_specs = (P(None, "gx", "gy", None), P(None, "gx"))
    return jax.shard_map(shards, mesh=mesh, in_specs=in_specs, out_specs=out_specs, check_vma=False)
```

```python
import jax
import jax.numpy as jnp
from jax import lax
from jax.experimental import pallas as pl
from jax.experimental.pallas import tpu as pltpu
from jax.sharding import PartitionSpec as P

MARKS = 128
CAPB = 2
SLOT_ROWS = 24
BACK_ROWS = 8
EDGE_ROWS = 24
SAMPLE_GROUP = 2
SAMPLE_UNROLL = 16
SPREAD_GROUP = 8
SPREAD_UNROLL = 4
CHUNK = 8


LATTICE = (
    (0, 0, 0),
    (1, 0, 0),
    (-1, 0, 0),
    (0, 1, 0),
    (0, -1, 0),
    (0, 0, 1),
    (0, 0, -1),
    (1, 1, 0),
    (-1, -1, 0),
    (1, -1, 0),
    (-1, 1, 0),
    (1, 0, 1),
    (-1, 0, -1),
    (1, 0, -1),
    (-1, 0, 1),
    (0, 1, 1),
    (0, -1, -1),
    (0, 1, -1),
    (0, -1, 1),
)
OPPOSITE = (0, 2, 1, 4, 3, 6, 5, 8, 7, 10, 9, 12, 11, 14, 13, 16, 15, 18, 17)
RELAX_TIME = 0.8
STIFFNESS = 2.0
MARKER_AREA = 1.0
BOND_SPRING = 1.0
BOND_DAMPING = 0.5
UP_X = tuple(i for i, v in enumerate(LATTICE) if v[0] == 1)
DOWN_X = tuple(i for i, v in enumerate(LATTICE) if v[0] == -1)
UP_Y = tuple(i for i, v in enumerate(LATTICE) if v[1] == 1)
DOWN_Y = tuple(i for i, v in enumerate(LATTICE) if v[1] == -1)
NT = (((1,), (1,)), ((), ()))
NN = (((1,), (0,)), ((), ()))
VMEM = pl.BlockSpec(memory_space=pltpu.VMEM)
SMEM = pl.BlockSpec(memory_space=pltpu.SMEM)
HBM = pl.BlockSpec(memory_space=pltpu.HBM)
F32 = jnp.float32
BF16 = jnp.bfloat16


def lattice_weight(vector):
    return (1.0 / 3.0, 1.0 / 18.0, 1.0 / 36.0)[abs(vector[0]) + abs(vector[1]) + abs(vector[2])]


def cross_rows(first_rows, second_rows):
    return [
        first_rows[1] * second_rows[2] - first_rows[2] * second_rows[1],
        first_rows[2] * second_rows[0] - first_rows[0] * second_rows[2],
        first_rows[0] * second_rows[1] - first_rows[1] * second_rows[0],
    ]


def rows_of(array):
    return [array[i : i + 1] for i in range(array.shape[0])]


def halves(value):
    high = value.astype(BF16)
    low = (value - high.astype(F32)).astype(BF16)
    return high, low


def is_even(place, axis, rows):
    return jnp.broadcast_to(place[8 * axis : 8 * axis + 1, :], (rows, place.shape[1])) == 0


def thirds(value):
    high = value.astype(BF16)
    rest = value - high.astype(F32)
    middle = rest.astype(BF16)
    return high, middle, (rest - middle.astype(F32)).astype(BF16)


def one_hot(count, index_row):
    lanes = index_row.shape[1]
    grid = lax.broadcasted_iota(jnp.int32, (count, lanes), 0)
    return jnp.where(grid == index_row, 1.0, 0.0).astype(BF16)


def pick(state, table, dims):
    rows = state.shape[0]
    stacked = jnp.concatenate([t.astype(F32) for t in thirds(state)], axis=0).astype(BF16)
    got = lax.dot_general(stacked, table, dims, preferred_element_type=F32)
    return got[:rows] + got[rows : 2 * rows] + got[2 * rows :]


def pad_rows(value, rows):
    return jnp.concatenate([value, jnp.zeros((rows - value.shape[0], value.shape[1]), F32)], axis=0)


def fetch(sources, targets, sems):
    copies = [
        pltpu.make_async_copy(source, target, sems.at[index])
        for index, (source, target) in enumerate(zip(sources, targets))
    ]
    for copy in copies:
        copy.start()
    return copies


def pack_kernel(*refs):
    sources, (out, used, sems), held = refs[:6], refs[6:9], refs[9:]
    copies = fetch(sources, held, sems)
    dest, grain, cell, motion, offset, weights = held
    blocks = grain.shape[0]
    slab = motion.shape[1]
    out[...] = jnp.zeros_like(out)
    for brick in range(out.shape[0]):
        used[brick] = 0
    for copy in copies:
        copy.wait()
    state = pad_rows(motion[...], 8)
    half = lax.broadcasted_iota(jnp.int32, (8, MARKS), 0) // 4
    for block in range(blocks):
        span = slice(block * MARKS, (block + 1) * MARKS)
        carried = pick(state, one_hot(slab, grain[block : block + 1, :]), NN)
        moved = rows_of(carried)
        lever = rows_of(offset[:, span])
        turned = cross_rows(moved[3:6], lever)
        tail = [moved[i] + turned[i] for i in range(3)]
        tail.append(cell[block : block + 1, :].astype(F32))
        tail = jnp.concatenate(tail + tail, axis=0)
        brick = dest[block]
        slot = used[brick]
        used[brick] = slot + 1
        out[brick, pl.ds(pl.multiple_of(8 * slot, 8), 8), :] = weights[:, span]
        out[brick, 16:24, :] = jnp.where(half == slot, tail, out[brick, 16:24, :])


def bond_part(pairs, rest, position, motion, bonded):
    slab = position.shape[1]
    state = pad_rows(jnp.concatenate([position[...], motion[0:3, :]], axis=0), 8)
    first = one_hot(slab, pairs[0:1, :])
    second = one_hot(slab, pairs[1:2, :])
    near = pick(state, first, NN)
    far = pick(state, second, NN)
    stretch = far[:3] - near[:3]
    force = BOND_SPRING * (stretch - rest[...]) + BOND_DAMPING * (far[3:6] - near[3:6])
    torque = [0.5 * row for row in cross_rows(rows_of(stretch), rows_of(force))]
    torque = jnp.concatenate(torque, axis=0)
    blank = jnp.zeros((2, force.shape[1]), F32)
    total = pick(jnp.concatenate([force, torque, blank], axis=0), first, NT)
    total = total + pick(jnp.concatenate([-force, torque, blank], axis=0), second, NT)
    bonded[...] = total


def momentum_of(current):
    total = []
    for axis in range(3):
        value = None
        for number, vector in enumerate(LATTICE):
            if vector[axis] == 0:
                continue
            if value is None:
                value = current[number] if vector[axis] == 1 else -current[number]
            elif vector[axis] == 1:
                value = value + current[number]
            else:
                value = value - current[number]
        total.append(value)
    return total


def sum_of(values):
    values = list(values)
    while len(values) > 1:
        values = [
            values[i] + values[i + 1] if i + 1 < len(values) else values[i]
            for i in range(0, len(values), 2)
        ]
    return values[0]


def moment_kernel(populations, pairs, rest, position, motion, table, bonded):
    quantity, size_x, size_y, size_z = populations.shape
    planes = size_x * size_y
    for x in range(size_x):
        current = [populations[q, x] for q in range(quantity)]
        inverse = 1.0 / sum_of(current)
        for axis, value in enumerate(momentum_of(current)):
            speed = value * inverse
            for step in range(2):
                if step == 1:
                    speed = pltpu.roll(speed, size_z - 1, 1)
                high, low = halves(speed)
                first = (step * 3 + axis) * planes + x * size_y
                table[first : first + size_y, 0:size_z] = high
                table[first : first + size_y, size_z : 2 * size_z] = low
    bond_part(pairs, rest, position, motion, bonded)


def marker_places(slots, size_x, size_y, size_z):
    cells = jnp.concatenate([slots[19:20], slots[23:24]], axis=1).astype(jnp.int32)
    weight = jnp.concatenate([slots[0:8], slots[8:16]], axis=1)
    place_x = lax.shift_right_logical(cells, (size_y * size_z).bit_length() - 1)
    place_y = lax.shift_right_logical(cells, size_z.bit_length() - 1) & (size_y - 1)
    place_z = cells & (size_z - 1)
    shares = []
    for x in range(size_x):
        share = jnp.where(place_x == x - 1, weight[4:8], 0.0)
        shares.append(jnp.where(place_x == x, weight[0:4], share))
    return shares, place_y, one_hot(size_z, place_z)


def marker_shares(shares, place_y, size_y):
    row = lax.broadcasted_iota(jnp.int32, (size_y, place_y.shape[1]), 0)
    at_low = row == place_y
    at_high = row == place_y + 1
    tables = [[], []]
    for share in shares:
        for corner in range(2):
            value = jnp.where(at_high, share[2 + corner : 3 + corner], 0.0)
            tables[corner].append(jnp.where(at_low, share[corner : corner + 1], value))
    return tables


def marker_halves(shares, place_y, size_y):
    at_low = one_hot(size_y, place_y)
    at_high = one_hot(size_y, place_y + 1)
    tables = [[], []]
    for part in range(2):
        split = [halves(share)[part] for share in shares]
        for corner in range(2):
            for share in split:
                low = at_low * share[corner : corner + 1]
                high = at_high * share[2 + corner : 3 + corner]
                tables[part].append(low + high)
    return [jnp.concatenate(table, axis=0) for table in tables]


def sample_kernel(slots, table, pushed, *, size):
    size_x, size_y, size_z = size
    planes = size_x * size_y

    def body(step, carry):
        tables = []
        for part in range(SAMPLE_GROUP):
            rows = slots[step * SAMPLE_GROUP + part]
            shares, place_y, depth = marker_places(rows, size_x, size_y, size_z)
            tables.append((rows, depth, marker_shares(shares, place_y, size_y)))
        depth = jnp.concatenate([entry[1] for entry in tables], axis=1)
        depth = jnp.concatenate([depth, depth], axis=0)
        found = lax.dot_general(table[...], depth, NN, preferred_element_type=F32)
        for part, (rows, _, shares) in enumerate(tables):
            span = slice(part * 2 * MARKS, (part + 1) * 2 * MARKS)
            target = jnp.concatenate([rows[16:19], rows[20:23]], axis=1)
            force = []
            for axis in range(3):
                value = None
                for corner in range(2):
                    for x in range(size_x):
                        first = (corner * 3 + axis) * planes + x * size_y
                        term = shares[corner][x] * found[first : first + size_y, span]
                        value = term if value is None else value + term
                sampled = jnp.sum(value, axis=0, keepdims=True)
                force.append(STIFFNESS * (target[axis : axis + 1] - sampled))
            blank = jnp.zeros_like(force[0])
            force = jnp.concatenate(force + [blank], axis=0)
            pushed[step * SAMPLE_GROUP + part] = jnp.concatenate(
                [force[:, :MARKS], force[:, MARKS:]], axis=0
            )
        return carry

    lax.fori_loop(0, slots.shape[0] // SAMPLE_GROUP, body, 0, unroll=SAMPLE_UNROLL)


def spread_kernel(
    place, slots, pushed, populations, collided, near_x, far_x, near_y, far_y, total
):
    quantity, size_x, size_y, size_z = populations.shape
    planes = size_x * size_y
    total[...] = jnp.zeros_like(total)

    def body(step, carry):
        wide, thin, strong, weak = [], [], [], []
        for part in range(SPREAD_GROUP):
            source = step * SPREAD_GROUP + part
            shares, place_y, depth = marker_places(slots[source], size_x, size_y, size_z)
            first, second = marker_halves(shares, place_y, size_y)
            both = pushed[source]
            force = MARKER_AREA * jnp.concatenate([both[0:4], both[4:8]], axis=1)
            high, low = halves(force)
            wide.append(first)
            thin.append(second)
            strong.append(jnp.concatenate([depth * high[a : a + 1] for a in range(3)], axis=0))
            weak.append(jnp.concatenate([depth * low[a : a + 1] for a in range(3)], axis=0))
        wide, thin, strong, weak = (
            jnp.concatenate(part, axis=1) for part in (wide, thin, strong, weak)
        )
        most = lax.dot_general(
            jnp.concatenate([strong, weak], axis=0), wide, NT, preferred_element_type=F32
        )
        rest = lax.dot_general(strong, thin, NT, preferred_element_type=F32)
        height = strong.shape[0]
        total[...] += most[:height] + (most[height:] + rest)
        return carry

    lax.fori_loop(0, slots.shape[0] // SPREAD_GROUP, body, 0, unroll=SPREAD_UNROLL)

    for axis in range(3):
        span = slice(axis * size_z, (axis + 1) * size_z)
        both = total[span, :planes] + pltpu.roll(total[span, planes:], 1, 0)
        total[span, :planes] = both.T

    factor = 1.0 - 0.5 / RELAX_TIME
    for x in range(size_x):
        for y in range(0, size_y, CHUNK):
            rows = slice(y, y + CHUNK)
            current = [populations[q, x, rows] for q in range(quantity)]
            density = sum_of(current)
            inverse = 1.0 / density
            momentum = momentum_of(current)
            forcing = []
            for axis in range(3):
                first = axis * size_z + x * size_y + y
                forcing.append(total[first : first + CHUNK, :size_z])
            flux = [momentum[a] + 0.5 * forcing[a] for a in range(3)]
            velocity = [flux[a] * inverse for a in range(3)]
            speed_square = sum_of([v * v for v in velocity])
            flow_force = sum_of([velocity[a] * forcing[a] for a in range(3)])
            flow_part = lattice_weight((1, 1, 0)) / RELAX_TIME
            force_part = factor * lattice_weight((1, 1, 0))
            base = (flow_part * density) * (1.0 - 1.5 * speed_square) - (
                3.0 * force_part
            ) * flow_force
            pushes = [(3.0 * force_part) * forcing[a] for a in range(3)]
            odd_field = [(3.0 * flow_part) * flux[a] + pushes[a] for a in range(3)]
            even_field = [odd_field[a] + pushes[a] for a in range(3)]
            speed = [1.5 * velocity[a] for a in range(3)]
            keep = 1.0 - 1.0 / RELAX_TIME
            for number, vector in enumerate(LATTICE):
                if OPPOSITE[number] < number:
                    continue
                if number == 0:
                    collided[0, x, rows] = keep * current[0] + 12.0 * base
                    continue
                odd = project(vector, odd_field)
                even = base + project(vector, speed) * project(vector, even_field)
                if number < 7:
                    odd = odd + odd
                    even = even + even
                other = OPPOSITE[number]
                collided[number, x, rows] = keep * current[number] + (even + odd)
                collided[other, x, rows] = keep * current[other] + (even - odd)

    even_x = is_even(place, 0, size_y)
    for index, (up, down) in enumerate(zip(UP_X, DOWN_X)):
        top = collided[up, size_x - 1]
        bottom = collided[down, 0]
        near_x[index] = jnp.where(even_x, top, bottom)
        far_x[index] = jnp.where(even_x, bottom, top)
    even_y = is_even(place, 1, 1)
    for index, (up, down) in enumerate(zip(UP_Y, DOWN_Y)):
        for x in range(size_x):
            top = collided[up, x, size_y - 1 : size_y]
            bottom = collided[down, x, 0:1]
            line = index * size_x + x
            near_y[line : line + 1] = jnp.where(even_y, top, bottom)
            far_y[line : line + 1] = jnp.where(even_y, bottom, top)
    filled = len(UP_Y) * size_x
    for face in (near_y, far_y):
        face[filled:] = jnp.zeros_like(face[filled:])


def edge_kernel(
    place, near_x, far_x, near_y, far_y, partial, across, near_out, far_out, total, *, size_x
):
    size_y = near_x.shape[1]
    filled = len(UP_Y) * size_x
    even_x = is_even(place, 0, 1)
    from_x = lambda number, y: jnp.where(
        even_x, far_x[UP_X.index(number), y : y + 1], near_x[UP_X.index(number), y : y + 1]
    )
    to_x = lambda number, y: jnp.where(
        even_x, near_x[DOWN_X.index(number), y : y + 1], far_x[DOWN_X.index(number), y : y + 1]
    )
    top = size_y - 1
    up = jnp.concatenate([from_x(LATTICE.index((1, 1, 0)), top), to_x(LATTICE.index((-1, 1, 0)), top)], axis=0)
    down = jnp.concatenate([from_x(LATTICE.index((1, -1, 0)), 0), to_x(LATTICE.index((-1, -1, 0)), 0)], axis=0)
    even_y = is_even(place, 1, 2)
    near_out[:EDGE_ROWS] = near_y[...]
    far_out[...] = far_y[...]
    width = near_out.shape[1]
    for part in range(partial.shape[1] // width):
        first = EDGE_ROWS + 8 * part
        span = slice(part * width, (part + 1) * width)
        value = partial[:, span] + across[:, span]
        total[:, span] = value
        near_out[first : first + 8] = value
    near_out[filled : filled + 2] = jnp.where(even_y, up, down)
    far_out[filled : filled + 2] = jnp.where(even_y, down, up)


def pair_kernel(partial, near_y, total):
    width = near_y.shape[1]
    for part in range(partial.shape[1] // width):
        first = EDGE_ROWS + 8 * part
        span = slice(part * width, (part + 1) * width)
        total[:, span] = partial[:, span] + near_y[first : first + 8]


def project(vector, field):
    value = None
    for axis in range(3):
        if vector[axis] == 0:
            continue
        if value is None:
            value = field[axis] if vector[axis] == 1 else -field[axis]
        elif vector[axis] == 1:
            value = value + field[axis]
        else:
            value = value - field[axis]
    return value


def stream_kernel(place, collided, near_x, far_x, near_y, far_y, out, stage, sems):
    quantity, size_x, size_y, size_z = collided.shape
    row = lax.broadcasted_iota(jnp.int32, (size_y, size_z), 0)
    lane = lax.broadcasted_iota(jnp.int32, (size_y, size_z), 1)
    even_x = is_even(place, 0, size_y)
    even_y = is_even(place, 1, EDGE_ROWS)
    filled = len(UP_Y) * size_x
    near, far = near_y[:EDGE_ROWS], far_y[...]
    from_y = jnp.where(even_y, far, near)
    to_y = jnp.where(even_y, near, far)
    copies = []
    for x in range(size_x):
        for number, vector in enumerate(LATTICE):
            source = x - vector[0]
            inside = 0 <= source < size_x
            if inside:
                value = collided[number, source]
            elif vector[0] == 1:
                index = UP_X.index(number)
                value = jnp.where(even_x, far_x[index], near_x[index])
            else:
                index = DOWN_X.index(number)
                value = jnp.where(even_x, near_x[index], far_x[index])
            if vector[1]:
                face = from_y if vector[1] == 1 else to_y
                column = UP_Y if vector[1] == 1 else DOWN_Y
                if inside:
                    line = column.index(number) * size_x + source
                else:
                    line = filled if vector[0] == 1 else filled + 1
                ghost = face[line : line + 1]
                if vector[1] == 1:
                    value = jnp.where(row == 0, ghost, pltpu.roll(value, 1, 0))
                else:
                    value = jnp.where(row == size_y - 1, ghost, pltpu.roll(value, size_y - 1, 0))
            if vector[2]:
                back = collided[OPPOSITE[number], x]
                if vector[2] == 1:
                    value = jnp.where(lane == 0, back, pltpu.roll(value, 1, 1))
                else:
                    value = jnp.where(lane == size_z - 1, back, pltpu.roll(value, size_z - 1, 1))
            stage[number, x] = value
        copy = pltpu.make_async_copy(stage.at[:, x], out.at[:, x], sems.at[x])
        copy.start()
        copies.append(copy)
    for copy in copies:
        copy.wait()


def load_kernel(bonded, first, second, load):
    total = first[...] + second[...] + bonded[...]
    load[...] = total[: load.shape[0]]


def grain_kernel(dest, grain, offset, returned, after, partial, used):
    blocks = grain.shape[0]
    slab = partial.shape[1]
    for brick in range(returned.shape[0]):
        used[brick] = 0
    total = None
    for block in range(blocks):
        span = slice(block * MARKS, (block + 1) * MARKS)
        brick = dest[block]
        slot = used[brick]
        used[brick] = slot + 1
        both = returned[brick]
        force = jnp.where(slot == 0, both[0:3], both[4:7])
        reaction = -MARKER_AREA * force
        torque = cross_rows(rows_of(offset[:, span]), rows_of(reaction))
        load = jnp.concatenate([reaction] + torque + [jnp.zeros((2, MARKS), F32)], axis=0)
        term = pick(load, one_hot(slab, grain[block : block + 1, :]), NT)
        total = term if total is None else total + term
    partial[...] = total


def cross(step):
    return [(i, i ^ step) for i in range(lax.axis_size("gy"))]


def swap(axis, step):
    count = lax.axis_size(axis)
    return [(i, (i + 1 if i % 2 == step else i - 1) % count) for i in range(count)]


def shards(
    populations,
    grain_position,
    grain_motion,
    marker_grain,
    marker_offset,
    marker_weights,
    marker_cell,
    block_dest,
    bond_pairs,
    bond_rest,
):
    quantity, size_x, size_y, size_z = populations.shape
    planes = size_x * size_y
    slab = grain_motion.shape[1]
    blocks = marker_grain.shape[0] // MARKS
    bricks = lax.axis_size("gx")
    shape = jax.ShapeDtypeStruct
    params = pltpu.CompilerParams(vmem_limit_bytes=48 * 1024 * 1024)
    grain_blocks = marker_grain.reshape(blocks, MARKS)
    cell_blocks = marker_cell.reshape(blocks, MARKS)

    place = jnp.concatenate(
        [jnp.full((8, size_z), lax.axis_index(axis) & 1, jnp.int32) for axis in ("gx", "gy")]
    )
    outgoing = pl.pallas_call(
        pack_kernel,
        out_shape=shape((bricks, SLOT_ROWS, MARKS), F32),
        in_specs=[HBM] * 6,
        out_specs=VMEM,
        scratch_shapes=[
            pltpu.SMEM((bricks,), jnp.int32),
            pltpu.SemaphoreType.DMA((6,)),
            pltpu.SMEM(block_dest.shape, jnp.int32),
            pltpu.VMEM(grain_blocks.shape, jnp.int32),
            pltpu.VMEM(cell_blocks.shape, jnp.int32),
            pltpu.VMEM(grain_motion.shape, F32),
            pltpu.VMEM(marker_offset.shape, F32),
            pltpu.VMEM(marker_weights.shape, F32),
        ],
        compiler_params=params,
        name="pack",
    )(
        *[
            pltpu.with_memory_space_constraint(array, pltpu.HBM)
            for array in (
                block_dest,
                grain_blocks,
                cell_blocks,
                grain_motion,
                marker_offset,
                marker_weights,
            )
        ]
    )
    slots = lax.all_to_all(outgoing, "gx", split_axis=0, concat_axis=0, tiled=True)

    table, bonded = pl.pallas_call(
        moment_kernel,
        out_shape=[shape((6 * planes, 2 * size_z), BF16), shape((8, slab), F32)],
        in_specs=[VMEM] * 5,
        out_specs=[VMEM] * 2,
        compiler_params=params,
        cost_estimate=pl.CostEstimate(flops=20000000, bytes_accessed=4000000, transcendentals=0),
        name="moments",
    )(populations, bond_pairs, bond_rest, grain_position, grain_motion)

    pushed = pl.pallas_call(
        lambda *refs: sample_kernel(*refs, size=(size_x, size_y, size_z)),
        out_shape=shape((bricks, BACK_ROWS, MARKS), F32),
        in_specs=[VMEM] * 2,
        out_specs=VMEM,
        compiler_params=params,
        name="sample",
    )(slots, table)
    returned = lax.all_to_all(pushed, "gx", split_axis=0, concat_axis=0, tiled=True)

    collided, *faces = pl.pallas_call(
        spread_kernel,
        out_shape=[
            shape(populations.shape, F32),
            shape((len(UP_X), size_y, size_z), F32),
            shape((len(UP_X), size_y, size_z), F32),
            shape((EDGE_ROWS, size_z), F32),
            shape((EDGE_ROWS, size_z), F32),
        ],
        in_specs=[VMEM] * 4,
        out_specs=[VMEM] * 5,
        scratch_shapes=[pltpu.VMEM((3 * size_z, 2 * planes), F32)],
        compiler_params=params,
        cost_estimate=pl.CostEstimate(
            flops=6000000000, bytes_accessed=8000000, transcendentals=0
        ),
        name="spread",
    )(place, slots, pushed, populations)

    partial = pl.pallas_call(
        grain_kernel,
        out_shape=shape((8, slab), F32),
        in_specs=[SMEM] + [VMEM] * 3 + [HBM],
        out_specs=VMEM,
        scratch_shapes=[pltpu.SMEM((bricks,), jnp.int32)],
        compiler_params=params,
        name="grain",
    )(block_dest, grain_blocks, marker_offset, returned, faces[2])
    near_x = lax.ppermute(faces[0], "gx", swap("gx", 0))
    far_x = lax.ppermute(faces[1], "gx", swap("gx", 1))
    across = lax.ppermute(partial, "gy", cross(4))
    near_y, far_y, total = pl.pallas_call(
        lambda *refs: edge_kernel(*refs, size_x=size_x),
        out_shape=[
            shape((EDGE_ROWS + 8 * slab // size_z, size_z), F32),
            shape((EDGE_ROWS, size_z), F32),
            shape((8, slab), F32),
        ],
        in_specs=[VMEM] * 7,
        out_specs=[VMEM] * 3,
        compiler_params=params,
        name="edge",
    )(place, near_x, far_x, faces[2], faces[3], partial, across)
    near_y = lax.ppermute(near_y, "gy", swap("gy", 0))
    far_y = lax.ppermute(far_y, "gy", swap("gy", 1))
    total = pl.pallas_call(
        pair_kernel,
        out_shape=shape((8, slab), F32),
        in_specs=[VMEM] * 2,
        out_specs=VMEM,
        compiler_params=params,
        name="pair",
    )(total, near_y)

    populations_next = pl.pallas_call(
        stream_kernel,
        out_shape=shape(populations.shape, F32),
        in_specs=[VMEM] * 6,
        out_specs=HBM,
        scratch_shapes=[
            pltpu.VMEM(populations.shape, F32),
            pltpu.SemaphoreType.DMA((size_x,)),
        ],
        compiler_params=params,
        cost_estimate=pl.CostEstimate(flops=20000000, bytes_accessed=4000000, transcendentals=0),
        name="stream",
    )(place, collided, near_x, far_x, near_y, far_y)

    grain_load = pl.pallas_call(
        load_kernel,
        out_shape=shape((6, slab), F32),
        in_specs=[VMEM] * 3,
        out_specs=VMEM,
        compiler_params=params,
        name="load",
    )(bonded, total, lax.ppermute(total, "gy", cross(2)))
    return populations_next, grain_load


def solution(mesh):
    in_specs = (
        P(None, "gx", "gy", None),
        P(None, "gx"),
        P(None, "gx"),
        P(("gx", "gy")),
        P(None, ("gx", "gy")),
        P(None, ("gx", "gy")),
        P(("gx", "gy")),
        P(("gx", "gy")),
        P(None, "gx"),
        P(None, "gx"),
    )
    out_specs = (P(None, "gx", "gy", None), P(None, "gx"))
    return jax.shard_map(shards, mesh=mesh, in_specs=in_specs, out_specs=out_specs, check_vma=False)
```

```python
import jax
import jax.numpy as jnp
from jax import lax
from jax.experimental import pallas as pl
from jax.experimental.pallas import tpu as pltpu
from jax.sharding import PartitionSpec as P

MARKS = 128
CAPB = 2
SLOT_ROWS = 24
BACK_ROWS = 8
EDGE_ROWS = 24
SAMPLE_GROUP = 2
SAMPLE_UNROLL = 16
SPREAD_GROUP = 8
SPREAD_FEW = 12
SPREAD_FEW_GROUP = 6
CHUNK = 8


LATTICE = (
    (0, 0, 0),
    (1, 0, 0),
    (-1, 0, 0),
    (0, 1, 0),
    (0, -1, 0),
    (0, 0, 1),
    (0, 0, -1),
    (1, 1, 0),
    (-1, -1, 0),
    (1, -1, 0),
    (-1, 1, 0),
    (1, 0, 1),
    (-1, 0, -1),
    (1, 0, -1),
    (-1, 0, 1),
    (0, 1, 1),
    (0, -1, -1),
    (0, 1, -1),
    (0, -1, 1),
)
OPPOSITE = (0, 2, 1, 4, 3, 6, 5, 8, 7, 10, 9, 12, 11, 14, 13, 16, 15, 18, 17)
RELAX_TIME = 0.8
STIFFNESS = 2.0
MARKER_AREA = 1.0
BOND_SPRING = 1.0
BOND_DAMPING = 0.5
UP_X = tuple(i for i, v in enumerate(LATTICE) if v[0] == 1)
DOWN_X = tuple(i for i, v in enumerate(LATTICE) if v[0] == -1)
UP_Y = tuple(i for i, v in enumerate(LATTICE) if v[1] == 1)
DOWN_Y = tuple(i for i, v in enumerate(LATTICE) if v[1] == -1)
NT = (((1,), (1,)), ((), ()))
NN = (((1,), (0,)), ((), ()))
VMEM = pl.BlockSpec(memory_space=pltpu.VMEM)
SMEM = pl.BlockSpec(memory_space=pltpu.SMEM)
HBM = pl.BlockSpec(memory_space=pltpu.HBM)
F32 = jnp.float32
BF16 = jnp.bfloat16


def lattice_weight(vector):
    return (1.0 / 3.0, 1.0 / 18.0, 1.0 / 36.0)[abs(vector[0]) + abs(vector[1]) + abs(vector[2])]


def cross_rows(first_rows, second_rows):
    return [
        first_rows[1] * second_rows[2] - first_rows[2] * second_rows[1],
        first_rows[2] * second_rows[0] - first_rows[0] * second_rows[2],
        first_rows[0] * second_rows[1] - first_rows[1] * second_rows[0],
    ]


def rows_of(array):
    return [array[i : i + 1] for i in range(array.shape[0])]


def halves(value):
    high = value.astype(BF16)
    low = (value - high.astype(F32)).astype(BF16)
    return high, low


def is_even(place, axis, rows):
    return jnp.broadcast_to(place[8 * axis : 8 * axis + 1, :], (rows, place.shape[1])) == 0


def thirds(value):
    high = value.astype(BF16)
    rest = value - high.astype(F32)
    middle = rest.astype(BF16)
    return high, middle, (rest - middle.astype(F32)).astype(BF16)


def one_hot(count, index_row):
    lanes = index_row.shape[1]
    grid = lax.broadcasted_iota(jnp.int32, (count, lanes), 0)
    return jnp.where(grid == index_row, 1.0, 0.0).astype(BF16)


def pick(state, table, dims):
    rows = state.shape[0]
    stacked = jnp.concatenate([t.astype(F32) for t in thirds(state)], axis=0).astype(BF16)
    got = lax.dot_general(stacked, table, dims, preferred_element_type=F32)
    return got[:rows] + got[rows : 2 * rows] + got[2 * rows :]


def pad_rows(value, rows):
    return jnp.concatenate([value, jnp.zeros((rows - value.shape[0], value.shape[1]), F32)], axis=0)


def fetch(sources, targets, sems):
    copies = [
        pltpu.make_async_copy(source, target, sems.at[index])
        for index, (source, target) in enumerate(zip(sources, targets))
    ]
    for copy in copies:
        copy.start()
    return copies


def pack_kernel(*refs):
    sources, (out, used, sems), held = refs[:6], refs[6:9], refs[9:]
    copies = fetch(sources, held, sems)
    dest, grain, cell, motion, offset, weights = held
    blocks = grain.shape[0]
    slab = motion.shape[1]
    out[...] = jnp.zeros_like(out)
    for brick in range(out.shape[0]):
        used[brick] = 0
    for copy in copies:
        copy.wait()
    state = pad_rows(motion[...], 8)
    half = lax.broadcasted_iota(jnp.int32, (8, MARKS), 0) // 4
    for block in range(blocks):
        span = slice(block * MARKS, (block + 1) * MARKS)
        carried = pick(state, one_hot(slab, grain[block : block + 1, :]), NN)
        moved = rows_of(carried)
        lever = rows_of(offset[:, span])
        turned = cross_rows(moved[3:6], lever)
        tail = [moved[i] + turned[i] for i in range(3)]
        tail.append(cell[block : block + 1, :].astype(F32))
        tail = jnp.concatenate(tail + tail, axis=0)
        brick = dest[block]
        slot = used[brick]
        used[brick] = slot + 1
        out[brick, pl.ds(pl.multiple_of(8 * slot, 8), 8), :] = weights[:, span]
        out[brick, 16:24, :] = jnp.where(half == slot, tail, out[brick, 16:24, :])


def bond_part(pairs, rest, position, motion, bonded):
    slab = position.shape[1]
    state = pad_rows(jnp.concatenate([position[...], motion[0:3, :]], axis=0), 8)
    first = one_hot(slab, pairs[0:1, :])
    second = one_hot(slab, pairs[1:2, :])
    near = pick(state, first, NN)
    far = pick(state, second, NN)
    stretch = far[:3] - near[:3]
    force = BOND_SPRING * (stretch - rest[...]) + BOND_DAMPING * (far[3:6] - near[3:6])
    torque = [0.5 * row for row in cross_rows(rows_of(stretch), rows_of(force))]
    torque = jnp.concatenate(torque, axis=0)
    blank = jnp.zeros((2, force.shape[1]), F32)
    total = pick(jnp.concatenate([force, torque, blank], axis=0), first, NT)
    total = total + pick(jnp.concatenate([-force, torque, blank], axis=0), second, NT)
    bonded[...] = total


def momentum_of(current):
    total = []
    for axis in range(3):
        value = None
        for number, vector in enumerate(LATTICE):
            if vector[axis] == 0:
                continue
            if value is None:
                value = current[number] if vector[axis] == 1 else -current[number]
            elif vector[axis] == 1:
                value = value + current[number]
            else:
                value = value - current[number]
        total.append(value)
    return total


def sum_of(values):
    values = list(values)
    while len(values) > 1:
        values = [
            values[i] + values[i + 1] if i + 1 < len(values) else values[i]
            for i in range(0, len(values), 2)
        ]
    return values[0]


def moment_kernel(populations, pairs, rest, position, motion, table, bonded):
    quantity, size_x, size_y, size_z = populations.shape
    planes = size_x * size_y
    for x in range(size_x):
        current = [populations[q, x] for q in range(quantity)]
        inverse = 1.0 / sum_of(current)
        for axis, value in enumerate(momentum_of(current)):
            speed = value * inverse
            for step in range(2):
                if step == 1:
                    speed = pltpu.roll(speed, size_z - 1, 1)
                high, low = halves(speed)
                first = (step * 3 + axis) * planes + x * size_y
                table[first : first + size_y, 0:size_z] = high
                table[first : first + size_y, size_z : 2 * size_z] = low
    bond_part(pairs, rest, position, motion, bonded)


def source_markers(slots):
    cells = jnp.concatenate([slots[19:20], slots[23:24]], axis=1).astype(jnp.int32)
    return cells, jnp.concatenate([slots[0:8], slots[8:16]], axis=1)


def marker_places(cells, weight, size_x, size_y, size_z):
    place_x = lax.shift_right_logical(cells, (size_y * size_z).bit_length() - 1)
    place_y = lax.shift_right_logical(cells, size_z.bit_length() - 1) & (size_y - 1)
    place_z = cells & (size_z - 1)
    shares = []
    for x in range(size_x):
        share = jnp.where(place_x == x - 1, weight[4:8], 0.0)
        shares.append(jnp.where(place_x == x, weight[0:4], share))
    return shares, place_y, one_hot(size_z, place_z)


def marker_shares(shares, place_y, size_y):
    row = lax.broadcasted_iota(jnp.int32, (size_y, place_y.shape[1]), 0)
    at_low = row == place_y
    at_high = row == place_y + 1
    tables = [[], []]
    for share in shares:
        for corner in range(2):
            value = jnp.where(at_high, share[2 + corner : 3 + corner], 0.0)
            tables[corner].append(jnp.where(at_low, share[corner : corner + 1], value))
    return tables


def marker_halves(shares, place_y, size_y):
    at_low = one_hot(size_y, place_y)
    at_high = one_hot(size_y, place_y + 1)
    tables = [[], []]
    for part in range(2):
        split = [halves(share)[part] for share in shares]
        for corner in range(2):
            for share in split:
                low = at_low * share[corner : corner + 1]
                high = at_high * share[2 + corner : 3 + corner]
                tables[part].append(low + high)
    return [jnp.concatenate(table, axis=0) for table in tables]


def sample_kernel(slots, table, pushed, filled, *, size):
    size_x, size_y, size_z = size
    planes = size_x * size_y

    def body(step, carry):
        tables = []
        for part in range(SAMPLE_GROUP):
            rows = slots[step * SAMPLE_GROUP + part]
            shares, place_y, depth = marker_places(*source_markers(rows), size_x, size_y, size_z)
            tables.append((rows, depth, marker_shares(shares, place_y, size_y)))
        depth = jnp.concatenate([entry[1] for entry in tables], axis=1)
        depth = jnp.concatenate([depth, depth], axis=0)
        found = lax.dot_general(table[...], depth, NN, preferred_element_type=F32)
        for part, (rows, _, shares) in enumerate(tables):
            span = slice(part * 2 * MARKS, (part + 1) * 2 * MARKS)
            target = jnp.concatenate([rows[16:19], rows[20:23]], axis=1)
            force = []
            for axis in range(3):
                value = None
                for corner in range(2):
                    for x in range(size_x):
                        first = (corner * 3 + axis) * planes + x * size_y
                        term = shares[corner][x] * found[first : first + size_y, span]
                        value = term if value is None else value + term
                sampled = jnp.sum(value, axis=0, keepdims=True)
                force.append(STIFFNESS * (target[axis : axis + 1] - sampled))
            blank = jnp.zeros_like(force[0])
            force = jnp.concatenate(force + [blank], axis=0)
            pushed[step * SAMPLE_GROUP + part] = jnp.concatenate(
                [force[:, :MARKS], force[:, MARKS:]], axis=0
            )
        return carry

    lax.fori_loop(0, slots.shape[0] // SAMPLE_GROUP, body, 0, unroll=SAMPLE_UNROLL)
    most = [
        jnp.max(slots[source, 8 * slot : 8 * slot + 8], axis=0, keepdims=True)
        for source in range(slots.shape[0])
        for slot in range(CAPB)
    ]
    most = jnp.max(jnp.concatenate(most, axis=0), axis=1, keepdims=True)
    filled[...] = jnp.broadcast_to(jnp.where(most > 0.0, 1, 0), filled.shape)


def spread_kernel(
    place,
    slots,
    pushed,
    filled,
    populations,
    collided,
    near_x,
    far_x,
    near_y,
    far_y,
    total,
    held,
    flags,
    order,
    sem,
):
    quantity, size_x, size_y, size_z = populations.shape
    planes = size_x * size_y
    copy = pltpu.make_async_copy(filled, flags, sem)
    copy.start()
    for x in range(size_x):
        for y in range(0, size_y, CHUNK):
            rows = slice(y, y + CHUNK)
            current = [populations[q, x, rows] for q in range(quantity)]
            density = sum_of(current)
            held[0, x, rows] = density
            held[1, x, rows] = 1.0 / density
            for axis, value in enumerate(momentum_of(current)):
                held[2 + axis, x, rows] = value

    def whole_source(source):
        both = pushed[source]
        force = jnp.concatenate([both[0:4], both[4:8]], axis=1)
        return (*source_markers(slots[source]), MARKER_AREA * force)

    def one_slot(index, scale):
        source = lax.shift_right_logical(index, 1)
        slot = index & 1
        weight = slots[source, pl.ds(pl.multiple_of(8 * slot, 8), 8), :]
        tail = slots[source, 16:24, :]
        both = pushed[source]
        cell = jnp.where(slot == 0, tail[3:4], tail[7:8]).astype(jnp.int32)
        return cell, weight, scale * jnp.where(slot == 0, both[0:4], both[4:8])

    def listed_pair(number):
        parts = []
        for which in (number * 2, number * 2 + 1):
            index = jnp.where(which < count, order[which], 0)
            parts.append(one_slot(index, jnp.where(which < count, MARKER_AREA, 0.0)))
        return tuple(jnp.concatenate(pair, axis=1) for pair in zip(*parts))

    def spread(markers):
        wide, thin, strong, weak = [], [], [], []
        for cells, weight, force in markers:
            shares, place_y, depth = marker_places(cells, weight, size_x, size_y, size_z)
            first, second = marker_halves(shares, place_y, size_y)
            high, low = halves(force)
            wide.append(first)
            thin.append(second)
            strong.append(jnp.concatenate([depth * high[a : a + 1] for a in range(3)], axis=0))
            weak.append(jnp.concatenate([depth * low[a : a + 1] for a in range(3)], axis=0))
        wide, thin, strong, weak = (
            jnp.concatenate(part, axis=1) for part in (wide, thin, strong, weak)
        )
        most = lax.dot_general(
            jnp.concatenate([strong, weak], axis=0), wide, NT, preferred_element_type=F32
        )
        rest = lax.dot_general(strong, thin, NT, preferred_element_type=F32)
        height = strong.shape[0]
        return most[:height] + (most[height:] + rest)

    def repeat(group, steps, markers):
        def body(step, carry):
            total[...] += spread([markers(step * group + part) for part in range(group)])
            return carry

        lax.fori_loop(0, steps, body, 0, unroll=steps)

    total[...] = jnp.zeros_like(total)
    copy.wait()
    count = jnp.int32(0)
    for slot in range(flags.shape[0]):
        order[count] = slot
        count = count + flags[slot, 0]

    @pl.when(count <= 2 * SPREAD_FEW)
    def _():
        repeat(SPREAD_FEW_GROUP, SPREAD_FEW // SPREAD_FEW_GROUP, listed_pair)

    @pl.when(count > 2 * SPREAD_FEW)
    def _():
        repeat(SPREAD_GROUP, slots.shape[0] // SPREAD_GROUP, whole_source)

    for axis in range(3):
        span = slice(axis * size_z, (axis + 1) * size_z)
        both = total[span, :planes] + pltpu.roll(total[span, planes:], 1, 0)
        total[span, :planes] = both.T

    factor = 1.0 - 0.5 / RELAX_TIME
    for x in range(size_x):
        for y in range(0, size_y, CHUNK):
            rows = slice(y, y + CHUNK)
            current = [populations[q, x, rows] for q in range(quantity)]
            density = held[0, x, rows]
            inverse = held[1, x, rows]
            momentum = [held[2 + axis, x, rows] for axis in range(3)]
            forcing = []
            for axis in range(3):
                first = axis * size_z + x * size_y + y
                forcing.append(total[first : first + CHUNK, :size_z])
            flux = [momentum[a] + 0.5 * forcing[a] for a in range(3)]
            velocity = [flux[a] * inverse for a in range(3)]
            speed_square = sum_of([v * v for v in velocity])
            flow_force = sum_of([velocity[a] * forcing[a] for a in range(3)])
            flow_part = lattice_weight((1, 1, 0)) / RELAX_TIME
            force_part = factor * lattice_weight((1, 1, 0))
            base = (flow_part * density) * (1.0 - 1.5 * speed_square) - (
                3.0 * force_part
            ) * flow_force
            pushes = [(3.0 * force_part) * forcing[a] for a in range(3)]
            odd_field = [(3.0 * flow_part) * flux[a] + pushes[a] for a in range(3)]
            even_field = [odd_field[a] + pushes[a] for a in range(3)]
            speed = [1.5 * velocity[a] for a in range(3)]
            keep = 1.0 - 1.0 / RELAX_TIME
            for number, vector in enumerate(LATTICE):
                if OPPOSITE[number] < number:
                    continue
                if number == 0:
                    collided[0, x, rows] = keep * current[0] + 12.0 * base
                    continue
                odd = project(vector, odd_field)
                even = base + project(vector, speed) * project(vector, even_field)
                if number < 7:
                    odd = odd + odd
                    even = even + even
                other = OPPOSITE[number]
                collided[number, x, rows] = keep * current[number] + (even + odd)
                collided[other, x, rows] = keep * current[other] + (even - odd)

    even_x = is_even(place, 0, size_y)
    for index, (up, down) in enumerate(zip(UP_X, DOWN_X)):
        top = collided[up, size_x - 1]
        bottom = collided[down, 0]
        near_x[index] = jnp.where(even_x, top, bottom)
        far_x[index] = jnp.where(even_x, bottom, top)
    even_y = is_even(place, 1, 1)
    for index, (up, down) in enumerate(zip(UP_Y, DOWN_Y)):
        for x in range(size_x):
            top = collided[up, x, size_y - 1 : size_y]
            bottom = collided[down, x, 0:1]
            line = index * size_x + x
            near_y[line : line + 1] = jnp.where(even_y, top, bottom)
            far_y[line : line + 1] = jnp.where(even_y, bottom, top)
    filled = len(UP_Y) * size_x
    for face in (near_y, far_y):
        face[filled:] = jnp.zeros_like(face[filled:])


def edge_kernel(
    place, near_x, far_x, near_y, far_y, partial, across, near_out, far_out, total, *, size_x
):
    size_y = near_x.shape[1]
    filled = len(UP_Y) * size_x
    even_x = is_even(place, 0, 1)
    from_x = lambda number, y: jnp.where(
        even_x, far_x[UP_X.index(number), y : y + 1], near_x[UP_X.index(number), y : y + 1]
    )
    to_x = lambda number, y: jnp.where(
        even_x, near_x[DOWN_X.index(number), y : y + 1], far_x[DOWN_X.index(number), y : y + 1]
    )
    top = size_y - 1
    up = jnp.concatenate([from_x(LATTICE.index((1, 1, 0)), top), to_x(LATTICE.index((-1, 1, 0)), top)], axis=0)
    down = jnp.concatenate([from_x(LATTICE.index((1, -1, 0)), 0), to_x(LATTICE.index((-1, -1, 0)), 0)], axis=0)
    even_y = is_even(place, 1, 2)
    near_out[:EDGE_ROWS] = near_y[...]
    far_out[...] = far_y[...]
    width = near_out.shape[1]
    for part in range(partial.shape[1] // width):
        first = EDGE_ROWS + 8 * part
        span = slice(part * width, (part + 1) * width)
        value = partial[:, span] + across[:, span]
        total[:, span] = value
        near_out[first : first + 8] = value
    near_out[filled : filled + 2] = jnp.where(even_y, up, down)
    far_out[filled : filled + 2] = jnp.where(even_y, down, up)


def pair_kernel(partial, near_y, total):
    width = near_y.shape[1]
    for part in range(partial.shape[1] // width):
        first = EDGE_ROWS + 8 * part
        span = slice(part * width, (part + 1) * width)
        total[:, span] = partial[:, span] + near_y[first : first + 8]


def project(vector, field):
    value = None
    for axis in range(3):
        if vector[axis] == 0:
            continue
        if value is None:
            value = field[axis] if vector[axis] == 1 else -field[axis]
        elif vector[axis] == 1:
            value = value + field[axis]
        else:
            value = value - field[axis]
    return value


def stream_kernel(place, collided, near_x, far_x, near_y, far_y, out, stage, sems):
    quantity, size_x, size_y, size_z = collided.shape
    row = lax.broadcasted_iota(jnp.int32, (size_y, size_z), 0)
    lane = lax.broadcasted_iota(jnp.int32, (size_y, size_z), 1)
    even_x = is_even(place, 0, size_y)
    even_y = is_even(place, 1, EDGE_ROWS)
    filled = len(UP_Y) * size_x
    near, far = near_y[:EDGE_ROWS], far_y[...]
    from_y = jnp.where(even_y, far, near)
    to_y = jnp.where(even_y, near, far)
    copies = []
    for x in range(size_x):
        for number, vector in enumerate(LATTICE):
            source = x - vector[0]
            inside = 0 <= source < size_x
            if inside:
                value = collided[number, source]
            elif vector[0] == 1:
                index = UP_X.index(number)
                value = jnp.where(even_x, far_x[index], near_x[index])
            else:
                index = DOWN_X.index(number)
                value = jnp.where(even_x, near_x[index], far_x[index])
            if vector[1]:
                face = from_y if vector[1] == 1 else to_y
                column = UP_Y if vector[1] == 1 else DOWN_Y
                if inside:
                    line = column.index(number) * size_x + source
                else:
                    line = filled if vector[0] == 1 else filled + 1
                ghost = face[line : line + 1]
                if vector[1] == 1:
                    value = jnp.where(row == 0, ghost, pltpu.roll(value, 1, 0))
                else:
                    value = jnp.where(row == size_y - 1, ghost, pltpu.roll(value, size_y - 1, 0))
            if vector[2]:
                back = collided[OPPOSITE[number], x]
                if vector[2] == 1:
                    value = jnp.where(lane == 0, back, pltpu.roll(value, 1, 1))
                else:
                    value = jnp.where(lane == size_z - 1, back, pltpu.roll(value, size_z - 1, 1))
            stage[number, x] = value
        copy = pltpu.make_async_copy(stage.at[:, x], out.at[:, x], sems.at[x])
        copy.start()
        copies.append(copy)
    for copy in copies:
        copy.wait()


def load_kernel(bonded, first, second, load):
    total = first[...] + second[...] + bonded[...]
    load[...] = total[: load.shape[0]]


def grain_kernel(dest, grain, offset, returned, after, partial, used):
    blocks = grain.shape[0]
    slab = partial.shape[1]
    for brick in range(returned.shape[0]):
        used[brick] = 0
    total = None
    for block in range(blocks):
        span = slice(block * MARKS, (block + 1) * MARKS)
        brick = dest[block]
        slot = used[brick]
        used[brick] = slot + 1
        both = returned[brick]
        force = jnp.where(slot == 0, both[0:3], both[4:7])
        reaction = -MARKER_AREA * force
        torque = cross_rows(rows_of(offset[:, span]), rows_of(reaction))
        load = jnp.concatenate([reaction] + torque + [jnp.zeros((2, MARKS), F32)], axis=0)
        term = pick(load, one_hot(slab, grain[block : block + 1, :]), NT)
        total = term if total is None else total + term
    partial[...] = total


def cross(step):
    return [(i, i ^ step) for i in range(lax.axis_size("gy"))]


def swap(axis, step):
    count = lax.axis_size(axis)
    return [(i, (i + 1 if i % 2 == step else i - 1) % count) for i in range(count)]


def shards(
    populations,
    grain_position,
    grain_motion,
    marker_grain,
    marker_offset,
    marker_weights,
    marker_cell,
    block_dest,
    bond_pairs,
    bond_rest,
):
    quantity, size_x, size_y, size_z = populations.shape
    planes = size_x * size_y
    slab = grain_motion.shape[1]
    blocks = marker_grain.shape[0] // MARKS
    bricks = lax.axis_size("gx")
    shape = jax.ShapeDtypeStruct
    params = pltpu.CompilerParams(vmem_limit_bytes=48 * 1024 * 1024)
    grain_blocks = marker_grain.reshape(blocks, MARKS)
    cell_blocks = marker_cell.reshape(blocks, MARKS)

    place = jnp.concatenate(
        [jnp.full((8, size_z), lax.axis_index(axis) & 1, jnp.int32) for axis in ("gx", "gy")]
    )
    outgoing = pl.pallas_call(
        pack_kernel,
        out_shape=shape((bricks, SLOT_ROWS, MARKS), F32),
        in_specs=[HBM] * 6,
        out_specs=VMEM,
        scratch_shapes=[
            pltpu.SMEM((bricks,), jnp.int32),
            pltpu.SemaphoreType.DMA((6,)),
            pltpu.SMEM(block_dest.shape, jnp.int32),
            pltpu.VMEM(grain_blocks.shape, jnp.int32),
            pltpu.VMEM(cell_blocks.shape, jnp.int32),
            pltpu.VMEM(grain_motion.shape, F32),
            pltpu.VMEM(marker_offset.shape, F32),
            pltpu.VMEM(marker_weights.shape, F32),
        ],
        compiler_params=params,
        name="pack",
    )(
        *[
            pltpu.with_memory_space_constraint(array, pltpu.HBM)
            for array in (
                block_dest,
                grain_blocks,
                cell_blocks,
                grain_motion,
                marker_offset,
                marker_weights,
            )
        ]
    )
    slots = lax.all_to_all(outgoing, "gx", split_axis=0, concat_axis=0, tiled=True)

    table, bonded = pl.pallas_call(
        moment_kernel,
        out_shape=[shape((6 * planes, 2 * size_z), BF16), shape((8, slab), F32)],
        in_specs=[VMEM] * 5,
        out_specs=[VMEM] * 2,
        compiler_params=params,
        cost_estimate=pl.CostEstimate(flops=20000000, bytes_accessed=4000000, transcendentals=0),
        name="moments",
    )(populations, bond_pairs, bond_rest, grain_position, grain_motion)

    pushed, filled = pl.pallas_call(
        lambda *refs: sample_kernel(*refs, size=(size_x, size_y, size_z)),
        out_shape=[
            shape((bricks, BACK_ROWS, MARKS), F32),
            shape((bricks * CAPB, MARKS), jnp.int32),
        ],
        in_specs=[VMEM] * 2,
        out_specs=[VMEM] * 2,
        compiler_params=params,
        name="sample",
    )(slots, table)
    returned = lax.all_to_all(pushed, "gx", split_axis=0, concat_axis=0, tiled=True)

    collided, *faces = pl.pallas_call(
        spread_kernel,
        out_shape=[
            shape(populations.shape, F32),
            shape((len(UP_X), size_y, size_z), F32),
            shape((len(UP_X), size_y, size_z), F32),
            shape((EDGE_ROWS, size_z), F32),
            shape((EDGE_ROWS, size_z), F32),
        ],
        in_specs=[VMEM] * 5,
        out_specs=[VMEM] * 5,
        scratch_shapes=[
            pltpu.VMEM((3 * size_z, 2 * planes), F32),
            pltpu.VMEM((5, size_x, size_y, size_z), F32),
            pltpu.SMEM((bricks * CAPB, MARKS), jnp.int32),
            pltpu.SMEM((bricks * CAPB + 1,), jnp.int32),
            pltpu.SemaphoreType.DMA,
        ],
        compiler_params=params,
        cost_estimate=pl.CostEstimate(
            flops=6000000000, bytes_accessed=8000000, transcendentals=0
        ),
        name="spread",
    )(place, slots, pushed, filled, populations)

    partial = pl.pallas_call(
        grain_kernel,
        out_shape=shape((8, slab), F32),
        in_specs=[SMEM] + [VMEM] * 3 + [HBM],
        out_specs=VMEM,
        scratch_shapes=[pltpu.SMEM((bricks,), jnp.int32)],
        compiler_params=params,
        name="grain",
    )(block_dest, grain_blocks, marker_offset, returned, faces[2])
    near_x = lax.ppermute(faces[0], "gx", swap("gx", 0))
    far_x = lax.ppermute(faces[1], "gx", swap("gx", 1))
    across = lax.ppermute(partial, "gy", cross(4))
    near_y, far_y, total = pl.pallas_call(
        lambda *refs: edge_kernel(*refs, size_x=size_x),
        out_shape=[
            shape((EDGE_ROWS + 8 * slab // size_z, size_z), F32),
            shape((EDGE_ROWS, size_z), F32),
            shape((8, slab), F32),
        ],
        in_specs=[VMEM] * 7,
        out_specs=[VMEM] * 3,
        compiler_params=params,
        name="edge",
    )(place, near_x, far_x, faces[2], faces[3], partial, across)
    near_y = lax.ppermute(near_y, "gy", swap("gy", 0))
    far_y = lax.ppermute(far_y, "gy", swap("gy", 1))
    total = pl.pallas_call(
        pair_kernel,
        out_shape=shape((8, slab), F32),
        in_specs=[VMEM] * 2,
        out_specs=VMEM,
        compiler_params=params,
        name="pair",
    )(total, near_y)

    populations_next = pl.pallas_call(
        stream_kernel,
        out_shape=shape(populations.shape, F32),
        in_specs=[VMEM] * 6,
        out_specs=HBM,
        scratch_shapes=[
            pltpu.VMEM(populations.shape, F32),
            pltpu.SemaphoreType.DMA((size_x,)),
        ],
        compiler_params=params,
        cost_estimate=pl.CostEstimate(flops=20000000, bytes_accessed=4000000, transcendentals=0),
        name="stream",
    )(place, collided, near_x, far_x, near_y, far_y)

    grain_load = pl.pallas_call(
        load_kernel,
        out_shape=shape((6, slab), F32),
        in_specs=[VMEM] * 3,
        out_specs=VMEM,
        compiler_params=params,
        name="load",
    )(bonded, total, lax.ppermute(total, "gy", cross(2)))
    return populations_next, grain_load


def solution(mesh):
    in_specs = (
        P(None, "gx", "gy", None),
        P(None, "gx"),
        P(None, "gx"),
        P(("gx", "gy")),
        P(None, ("gx", "gy")),
        P(None, ("gx", "gy")),
        P(("gx", "gy")),
        P(("gx", "gy")),
        P(None, "gx"),
        P(None, "gx"),
    )
    out_specs = (P(None, "gx", "gy", None), P(None, "gx"))
    return jax.shard_map(shards, mesh=mesh, in_specs=in_specs, out_specs=out_specs, check_vma=False)
```

```python
import jax
import jax.numpy as jnp
from jax import lax
from jax.experimental import pallas as pl
from jax.experimental.pallas import tpu as pltpu
from jax.sharding import PartitionSpec as P

MARKS = 128
CAPB = 2
SLOT_ROWS = 24
BACK_ROWS = 8
EDGE_ROWS = 24
SAMPLE_GROUP = 2
SAMPLE_UNROLL = 16
SPREAD_GROUP = 8
SPREAD_FEW = 14
SPREAD_FEW_GROUP = 7
CHUNK = 8


LATTICE = (
    (0, 0, 0),
    (1, 0, 0),
    (-1, 0, 0),
    (0, 1, 0),
    (0, -1, 0),
    (0, 0, 1),
    (0, 0, -1),
    (1, 1, 0),
    (-1, -1, 0),
    (1, -1, 0),
    (-1, 1, 0),
    (1, 0, 1),
    (-1, 0, -1),
    (1, 0, -1),
    (-1, 0, 1),
    (0, 1, 1),
    (0, -1, -1),
    (0, 1, -1),
    (0, -1, 1),
)
OPPOSITE = (0, 2, 1, 4, 3, 6, 5, 8, 7, 10, 9, 12, 11, 14, 13, 16, 15, 18, 17)
RELAX_TIME = 0.8
STIFFNESS = 2.0
MARKER_AREA = 1.0
BOND_SPRING = 1.0
BOND_DAMPING = 0.5
UP_X = tuple(i for i, v in enumerate(LATTICE) if v[0] == 1)
DOWN_X = tuple(i for i, v in enumerate(LATTICE) if v[0] == -1)
UP_Y = tuple(i for i, v in enumerate(LATTICE) if v[1] == 1)
DOWN_Y = tuple(i for i, v in enumerate(LATTICE) if v[1] == -1)
NT = (((1,), (1,)), ((), ()))
NN = (((1,), (0,)), ((), ()))
VMEM = pl.BlockSpec(memory_space=pltpu.VMEM)
SMEM = pl.BlockSpec(memory_space=pltpu.SMEM)
HBM = pl.BlockSpec(memory_space=pltpu.HBM)
F32 = jnp.float32
BF16 = jnp.bfloat16


def lattice_weight(vector):
    return (1.0 / 3.0, 1.0 / 18.0, 1.0 / 36.0)[abs(vector[0]) + abs(vector[1]) + abs(vector[2])]


def cross_rows(first_rows, second_rows):
    return [
        first_rows[1] * second_rows[2] - first_rows[2] * second_rows[1],
        first_rows[2] * second_rows[0] - first_rows[0] * second_rows[2],
        first_rows[0] * second_rows[1] - first_rows[1] * second_rows[0],
    ]


def rows_of(array):
    return [array[i : i + 1] for i in range(array.shape[0])]


def halves(value):
    high = value.astype(BF16)
    low = (value - high.astype(F32)).astype(BF16)
    return high, low


def is_even(place, axis, rows):
    return jnp.broadcast_to(place[8 * axis : 8 * axis + 1, :], (rows, place.shape[1])) == 0


def thirds(value):
    high = value.astype(BF16)
    rest = value - high.astype(F32)
    middle = rest.astype(BF16)
    return high, middle, (rest - middle.astype(F32)).astype(BF16)


def one_hot(count, index_row):
    lanes = index_row.shape[1]
    grid = lax.broadcasted_iota(jnp.int32, (count, lanes), 0)
    return jnp.where(grid == index_row, 1.0, 0.0).astype(BF16)


def pick(state, table, dims):
    rows = state.shape[0]
    stacked = jnp.concatenate([t.astype(F32) for t in thirds(state)], axis=0).astype(BF16)
    got = lax.dot_general(stacked, table, dims, preferred_element_type=F32)
    return got[:rows] + got[rows : 2 * rows] + got[2 * rows :]


def pad_rows(value, rows):
    return jnp.concatenate([value, jnp.zeros((rows - value.shape[0], value.shape[1]), F32)], axis=0)


def fetch(sources, targets, sems):
    copies = [
        pltpu.make_async_copy(source, target, sems.at[index])
        for index, (source, target) in enumerate(zip(sources, targets))
    ]
    for copy in copies:
        copy.start()
    return copies


def pack_kernel(*refs):
    sources, (out, used, sems), held = refs[:6], refs[6:9], refs[9:]
    copies = fetch(sources, held, sems)
    dest, grain, cell, motion, offset, weights = held
    blocks = grain.shape[0]
    slab = motion.shape[1]
    out[...] = jnp.zeros_like(out)
    for brick in range(out.shape[0]):
        used[brick] = 0
    for copy in copies:
        copy.wait()
    state = pad_rows(motion[...], 8)
    half = lax.broadcasted_iota(jnp.int32, (8, MARKS), 0) // 4
    for block in range(blocks):
        span = slice(block * MARKS, (block + 1) * MARKS)
        carried = pick(state, one_hot(slab, grain[block : block + 1, :]), NN)
        moved = rows_of(carried)
        lever = rows_of(offset[:, span])
        turned = cross_rows(moved[3:6], lever)
        tail = [moved[i] + turned[i] for i in range(3)]
        tail.append(cell[block : block + 1, :].astype(F32))
        tail = jnp.concatenate(tail + tail, axis=0)
        brick = dest[block]
        slot = used[brick]
        used[brick] = slot + 1
        out[brick, pl.ds(pl.multiple_of(8 * slot, 8), 8), :] = weights[:, span]
        out[brick, 16:24, :] = jnp.where(half == slot, tail, out[brick, 16:24, :])


def bond_part(pairs, rest, position, motion, bonded):
    slab = position.shape[1]
    state = pad_rows(jnp.concatenate([position[...], motion[0:3, :]], axis=0), 8)
    first = one_hot(slab, pairs[0:1, :])
    second = one_hot(slab, pairs[1:2, :])
    near = pick(state, first, NN)
    far = pick(state, second, NN)
    stretch = far[:3] - near[:3]
    force = BOND_SPRING * (stretch - rest[...]) + BOND_DAMPING * (far[3:6] - near[3:6])
    torque = [0.5 * row for row in cross_rows(rows_of(stretch), rows_of(force))]
    torque = jnp.concatenate(torque, axis=0)
    blank = jnp.zeros((2, force.shape[1]), F32)
    total = pick(jnp.concatenate([force, torque, blank], axis=0), first, NT)
    total = total + pick(jnp.concatenate([-force, torque, blank], axis=0), second, NT)
    bonded[...] = total


def momentum_of(current):
    total = []
    for axis in range(3):
        value = None
        for number, vector in enumerate(LATTICE):
            if vector[axis] == 0:
                continue
            if value is None:
                value = current[number] if vector[axis] == 1 else -current[number]
            elif vector[axis] == 1:
                value = value + current[number]
            else:
                value = value - current[number]
        total.append(value)
    return total


def sum_of(values):
    values = list(values)
    while len(values) > 1:
        values = [
            values[i] + values[i + 1] if i + 1 < len(values) else values[i]
            for i in range(0, len(values), 2)
        ]
    return values[0]


def moment_kernel(populations, pairs, rest, position, motion, table, bonded):
    quantity, size_x, size_y, size_z = populations.shape
    planes = size_x * size_y
    for x in range(size_x):
        current = [populations[q, x] for q in range(quantity)]
        inverse = 1.0 / sum_of(current)
        for axis, value in enumerate(momentum_of(current)):
            speed = value * inverse
            for step in range(2):
                if step == 1:
                    speed = pltpu.roll(speed, size_z - 1, 1)
                high, low = halves(speed)
                first = (step * 3 + axis) * planes + x * size_y
                table[first : first + size_y, 0:size_z] = high
                table[first : first + size_y, size_z : 2 * size_z] = low
    bond_part(pairs, rest, position, motion, bonded)


def source_markers(slots):
    cells = jnp.concatenate([slots[19:20], slots[23:24]], axis=1).astype(jnp.int32)
    return cells, jnp.concatenate([slots[0:8], slots[8:16]], axis=1)


def marker_places(cells, weight, size_x, size_y, size_z):
    place_x = lax.shift_right_logical(cells, (size_y * size_z).bit_length() - 1)
    place_y = lax.shift_right_logical(cells, size_z.bit_length() - 1) & (size_y - 1)
    place_z = cells & (size_z - 1)
    shares = []
    for x in range(size_x):
        share = jnp.where(place_x == x - 1, weight[4:8], 0.0)
        shares.append(jnp.where(place_x == x, weight[0:4], share))
    return shares, place_y, one_hot(size_z, place_z)


def marker_shares(shares, place_y, size_y):
    row = lax.broadcasted_iota(jnp.int32, (size_y, place_y.shape[1]), 0)
    at_low = row == place_y
    at_high = row == place_y + 1
    tables = [[], []]
    for share in shares:
        for corner in range(2):
            value = jnp.where(at_high, share[2 + corner : 3 + corner], 0.0)
            tables[corner].append(jnp.where(at_low, share[corner : corner + 1], value))
    return tables


def marker_halves(shares, place_y, size_y):
    at_low = one_hot(size_y, place_y)
    at_high = one_hot(size_y, place_y + 1)
    tables = [[], []]
    for part in range(2):
        split = [halves(share)[part] for share in shares]
        for corner in range(2):
            for share in split:
                low = at_low * share[corner : corner + 1]
                high = at_high * share[2 + corner : 3 + corner]
                tables[part].append(low + high)
    return [jnp.concatenate(table, axis=0) for table in tables]


def sample_kernel(slots, table, pushed, filled, *, size):
    size_x, size_y, size_z = size
    planes = size_x * size_y

    def body(step, carry):
        tables = []
        for part in range(SAMPLE_GROUP):
            rows = slots[step * SAMPLE_GROUP + part]
            shares, place_y, depth = marker_places(*source_markers(rows), size_x, size_y, size_z)
            tables.append((rows, depth, marker_shares(shares, place_y, size_y)))
        depth = jnp.concatenate([entry[1] for entry in tables], axis=1)
        depth = jnp.concatenate([depth, depth], axis=0)
        found = lax.dot_general(table[...], depth, NN, preferred_element_type=F32)
        for part, (rows, _, shares) in enumerate(tables):
            span = slice(part * 2 * MARKS, (part + 1) * 2 * MARKS)
            target = jnp.concatenate([rows[16:19], rows[20:23]], axis=1)
            force = []
            for axis in range(3):
                value = None
                for corner in range(2):
                    for x in range(size_x):
                        first = (corner * 3 + axis) * planes + x * size_y
                        term = shares[corner][x] * found[first : first + size_y, span]
                        value = term if value is None else value + term
                sampled = jnp.sum(value, axis=0, keepdims=True)
                force.append(STIFFNESS * (target[axis : axis + 1] - sampled))
            blank = jnp.zeros_like(force[0])
            force = jnp.concatenate(force + [blank], axis=0)
            pushed[step * SAMPLE_GROUP + part] = jnp.concatenate(
                [force[:, :MARKS], force[:, MARKS:]], axis=0
            )
        return carry

    lax.fori_loop(0, slots.shape[0] // SAMPLE_GROUP, body, 0, unroll=SAMPLE_UNROLL)
    most = [
        jnp.max(slots[source, 8 * slot : 8 * slot + 8], axis=0, keepdims=True)
        for source in range(slots.shape[0])
        for slot in range(CAPB)
    ]
    most = jnp.max(jnp.concatenate(most, axis=0), axis=1, keepdims=True)
    filled[...] = jnp.broadcast_to(jnp.where(most > 0.0, 1, 0), filled.shape)


def spread_kernel(
    place,
    slots,
    pushed,
    filled,
    populations,
    collided,
    near_x,
    far_x,
    near_y,
    far_y,
    total,
    held,
    flags,
    order,
    sem,
):
    quantity, size_x, size_y, size_z = populations.shape
    planes = size_x * size_y
    copy = pltpu.make_async_copy(filled, flags, sem)
    copy.start()
    for x in range(size_x):
        for y in range(0, size_y, CHUNK):
            rows = slice(y, y + CHUNK)
            current = [populations[q, x, rows] for q in range(quantity)]
            density = sum_of(current)
            held[0, x, rows] = density
            held[1, x, rows] = 1.0 / density
            for axis, value in enumerate(momentum_of(current)):
                held[2 + axis, x, rows] = value

    def whole_source(source):
        both = pushed[source]
        force = jnp.concatenate([both[0:4], both[4:8]], axis=1)
        return (*source_markers(slots[source]), MARKER_AREA * force)

    def one_slot(index, scale):
        source = lax.shift_right_logical(index, 1)
        slot = index & 1
        weight = slots[source, pl.ds(pl.multiple_of(8 * slot, 8), 8), :]
        tail = slots[source, 16:24, :]
        both = pushed[source]
        cell = jnp.where(slot == 0, tail[3:4], tail[7:8]).astype(jnp.int32)
        return cell, weight, scale * jnp.where(slot == 0, both[0:4], both[4:8])

    def listed_pair(number):
        parts = []
        for which in (number * 2, number * 2 + 1):
            index = jnp.where(which < count, order[which], 0)
            parts.append(one_slot(index, jnp.where(which < count, MARKER_AREA, 0.0)))
        return tuple(jnp.concatenate(pair, axis=1) for pair in zip(*parts))

    def spread(markers):
        wide, thin, strong, weak = [], [], [], []
        for cells, weight, force in markers:
            shares, place_y, depth = marker_places(cells, weight, size_x, size_y, size_z)
            first, second = marker_halves(shares, place_y, size_y)
            high, low = halves(force)
            wide.append(first)
            thin.append(second)
            strong.append(jnp.concatenate([depth * high[a : a + 1] for a in range(3)], axis=0))
            weak.append(jnp.concatenate([depth * low[a : a + 1] for a in range(3)], axis=0))
        wide, thin, strong, weak = (
            jnp.concatenate(part, axis=1) for part in (wide, thin, strong, weak)
        )
        most = lax.dot_general(
            jnp.concatenate([strong, weak], axis=0), wide, NT, preferred_element_type=F32
        )
        rest = lax.dot_general(strong, thin, NT, preferred_element_type=F32)
        height = strong.shape[0]
        return most[:height] + (most[height:] + rest)

    def repeat(group, steps, markers):
        def body(step, carry):
            total[...] += spread([markers(step * group + part) for part in range(group)])
            return carry

        lax.fori_loop(0, steps, body, 0, unroll=steps)

    total[...] = jnp.zeros_like(total)
    copy.wait()
    count = jnp.int32(0)
    for slot in range(flags.shape[0]):
        order[count] = slot
        count = count + flags[slot, 0]

    @pl.when(count <= 2 * SPREAD_FEW)
    def _():
        repeat(SPREAD_FEW_GROUP, SPREAD_FEW // SPREAD_FEW_GROUP, listed_pair)

    @pl.when(count > 2 * SPREAD_FEW)
    def _():
        repeat(SPREAD_GROUP, slots.shape[0] // SPREAD_GROUP, whole_source)

    for axis in range(3):
        span = slice(axis * size_z, (axis + 1) * size_z)
        both = total[span, :planes] + pltpu.roll(total[span, planes:], 1, 0)
        total[span, :planes] = both.T

    factor = 1.0 - 0.5 / RELAX_TIME
    for x in range(size_x):
        for y in range(0, size_y, CHUNK):
            rows = slice(y, y + CHUNK)
            current = [populations[q, x, rows] for q in range(quantity)]
            density = held[0, x, rows]
            inverse = held[1, x, rows]
            momentum = [held[2 + axis, x, rows] for axis in range(3)]
            forcing = []
            for axis in range(3):
                first = axis * size_z + x * size_y + y
                forcing.append(total[first : first + CHUNK, :size_z])
            flux = [momentum[a] + 0.5 * forcing[a] for a in range(3)]
            velocity = [flux[a] * inverse for a in range(3)]
            speed_square = sum_of([v * v for v in velocity])
            flow_force = sum_of([velocity[a] * forcing[a] for a in range(3)])
            flow_part = lattice_weight((1, 1, 0)) / RELAX_TIME
            force_part = factor * lattice_weight((1, 1, 0))
            base = (flow_part * density) * (1.0 - 1.5 * speed_square) - (
                3.0 * force_part
            ) * flow_force
            pushes = [(3.0 * force_part) * forcing[a] for a in range(3)]
            odd_field = [(3.0 * flow_part) * flux[a] + pushes[a] for a in range(3)]
            even_field = [odd_field[a] + pushes[a] for a in range(3)]
            speed = [1.5 * velocity[a] for a in range(3)]
            keep = 1.0 - 1.0 / RELAX_TIME
            for number, vector in enumerate(LATTICE):
                if OPPOSITE[number] < number:
                    continue
                if number == 0:
                    collided[0, x, rows] = keep * current[0] + 12.0 * base
                    continue
                odd = project(vector, odd_field)
                even = base + project(vector, speed) * project(vector, even_field)
                if number < 7:
                    odd = odd + odd
                    even = even + even
                other = OPPOSITE[number]
                collided[number, x, rows] = keep * current[number] + (even + odd)
                collided[other, x, rows] = keep * current[other] + (even - odd)

    even_x = is_even(place, 0, size_y)
    for index, (up, down) in enumerate(zip(UP_X, DOWN_X)):
        top = collided[up, size_x - 1]
        bottom = collided[down, 0]
        near_x[index] = jnp.where(even_x, top, bottom)
        far_x[index] = jnp.where(even_x, bottom, top)
    even_y = is_even(place, 1, 1)
    for index, (up, down) in enumerate(zip(UP_Y, DOWN_Y)):
        for x in range(size_x):
            top = collided[up, x, size_y - 1 : size_y]
            bottom = collided[down, x, 0:1]
            line = index * size_x + x
            near_y[line : line + 1] = jnp.where(even_y, top, bottom)
            far_y[line : line + 1] = jnp.where(even_y, bottom, top)
    filled = len(UP_Y) * size_x
    for face in (near_y, far_y):
        face[filled:] = jnp.zeros_like(face[filled:])


def edge_kernel(
    place, near_x, far_x, near_y, far_y, partial, across, near_out, far_out, total, *, size_x
):
    size_y = near_x.shape[1]
    filled = len(UP_Y) * size_x
    even_x = is_even(place, 0, 1)
    from_x = lambda number, y: jnp.where(
        even_x, far_x[UP_X.index(number), y : y + 1], near_x[UP_X.index(number), y : y + 1]
    )
    to_x = lambda number, y: jnp.where(
        even_x, near_x[DOWN_X.index(number), y : y + 1], far_x[DOWN_X.index(number), y : y + 1]
    )
    top = size_y - 1
    up = jnp.concatenate([from_x(LATTICE.index((1, 1, 0)), top), to_x(LATTICE.index((-1, 1, 0)), top)], axis=0)
    down = jnp.concatenate([from_x(LATTICE.index((1, -1, 0)), 0), to_x(LATTICE.index((-1, -1, 0)), 0)], axis=0)
    even_y = is_even(place, 1, 2)
    near_out[:EDGE_ROWS] = near_y[...]
    far_out[...] = far_y[...]
    width = near_out.shape[1]
    for part in range(partial.shape[1] // width):
        first = EDGE_ROWS + 8 * part
        span = slice(part * width, (part + 1) * width)
        value = partial[:, span] + across[:, span]
        total[:, span] = value
        near_out[first : first + 8] = value
    near_out[filled : filled + 2] = jnp.where(even_y, up, down)
    far_out[filled : filled + 2] = jnp.where(even_y, down, up)


def pair_kernel(partial, near_y, total):
    width = near_y.shape[1]
    for part in range(partial.shape[1] // width):
        first = EDGE_ROWS + 8 * part
        span = slice(part * width, (part + 1) * width)
        total[:, span] = partial[:, span] + near_y[first : first + 8]


def project(vector, field):
    value = None
    for axis in range(3):
        if vector[axis] == 0:
            continue
        if value is None:
            value = field[axis] if vector[axis] == 1 else -field[axis]
        elif vector[axis] == 1:
            value = value + field[axis]
        else:
            value = value - field[axis]
    return value


def stream_kernel(place, collided, near_x, far_x, near_y, far_y, out, stage, sems):
    quantity, size_x, size_y, size_z = collided.shape
    row = lax.broadcasted_iota(jnp.int32, (size_y, size_z), 0)
    lane = lax.broadcasted_iota(jnp.int32, (size_y, size_z), 1)
    even_x = is_even(place, 0, size_y)
    even_y = is_even(place, 1, EDGE_ROWS)
    filled = len(UP_Y) * size_x
    near, far = near_y[:EDGE_ROWS], far_y[...]
    from_y = jnp.where(even_y, far, near)
    to_y = jnp.where(even_y, near, far)
    copies = []
    for x in range(size_x):
        for number, vector in enumerate(LATTICE):
            source = x - vector[0]
            inside = 0 <= source < size_x
            if inside:
                value = collided[number, source]
            elif vector[0] == 1:
                index = UP_X.index(number)
                value = jnp.where(even_x, far_x[index], near_x[index])
            else:
                index = DOWN_X.index(number)
                value = jnp.where(even_x, near_x[index], far_x[index])
            if vector[1]:
                face = from_y if vector[1] == 1 else to_y
                column = UP_Y if vector[1] == 1 else DOWN_Y
                if inside:
                    line = column.index(number) * size_x + source
                else:
                    line = filled if vector[0] == 1 else filled + 1
                ghost = face[line : line + 1]
                if vector[1] == 1:
                    value = jnp.where(row == 0, ghost, pltpu.roll(value, 1, 0))
                else:
                    value = jnp.where(row == size_y - 1, ghost, pltpu.roll(value, size_y - 1, 0))
            if vector[2]:
                back = collided[OPPOSITE[number], x]
                if vector[2] == 1:
                    value = jnp.where(lane == 0, back, pltpu.roll(value, 1, 1))
                else:
                    value = jnp.where(lane == size_z - 1, back, pltpu.roll(value, size_z - 1, 1))
            stage[number, x] = value
        copy = pltpu.make_async_copy(stage.at[:, x], out.at[:, x], sems.at[x])
        copy.start()
        copies.append(copy)
    for copy in copies:
        copy.wait()


def load_kernel(bonded, first, second, load):
    total = first[...] + second[...] + bonded[...]
    load[...] = total[: load.shape[0]]


def grain_kernel(dest, grain, offset, returned, face, partial, passed, used):
    passed[...] = face[...]
    blocks = grain.shape[0]
    slab = partial.shape[1]
    for brick in range(returned.shape[0]):
        used[brick] = 0
    total = None
    for block in range(blocks):
        span = slice(block * MARKS, (block + 1) * MARKS)
        brick = dest[block]
        slot = used[brick]
        used[brick] = slot + 1
        both = returned[brick]
        force = jnp.where(slot == 0, both[0:3], both[4:7])
        reaction = -MARKER_AREA * force
        torque = cross_rows(rows_of(offset[:, span]), rows_of(reaction))
        load = jnp.concatenate([reaction] + torque + [jnp.zeros((2, MARKS), F32)], axis=0)
        term = pick(load, one_hot(slab, grain[block : block + 1, :]), NT)
        total = term if total is None else total + term
    partial[...] = total


def cross(step):
    return [(i, i ^ step) for i in range(lax.axis_size("gy"))]


def swap(axis, step):
    count = lax.axis_size(axis)
    return [(i, (i + 1 if i % 2 == step else i - 1) % count) for i in range(count)]


def shards(
    populations,
    grain_position,
    grain_motion,
    marker_grain,
    marker_offset,
    marker_weights,
    marker_cell,
    block_dest,
    bond_pairs,
    bond_rest,
):
    quantity, size_x, size_y, size_z = populations.shape
    planes = size_x * size_y
    slab = grain_motion.shape[1]
    blocks = marker_grain.shape[0] // MARKS
    bricks = lax.axis_size("gx")
    shape = jax.ShapeDtypeStruct
    params = pltpu.CompilerParams(vmem_limit_bytes=48 * 1024 * 1024)
    grain_blocks = marker_grain.reshape(blocks, MARKS)
    cell_blocks = marker_cell.reshape(blocks, MARKS)

    place = jnp.concatenate(
        [jnp.full((8, size_z), lax.axis_index(axis) & 1, jnp.int32) for axis in ("gx", "gy")]
    )
    outgoing = pl.pallas_call(
        pack_kernel,
        out_shape=shape((bricks, SLOT_ROWS, MARKS), F32),
        in_specs=[HBM] * 6,
        out_specs=VMEM,
        scratch_shapes=[
            pltpu.SMEM((bricks,), jnp.int32),
            pltpu.SemaphoreType.DMA((6,)),
            pltpu.SMEM(block_dest.shape, jnp.int32),
            pltpu.VMEM(grain_blocks.shape, jnp.int32),
            pltpu.VMEM(cell_blocks.shape, jnp.int32),
            pltpu.VMEM(grain_motion.shape, F32),
            pltpu.VMEM(marker_offset.shape, F32),
            pltpu.VMEM(marker_weights.shape, F32),
        ],
        compiler_params=params,
        name="pack",
    )(
        *[
            pltpu.with_memory_space_constraint(array, pltpu.HBM)
            for array in (
                block_dest,
                grain_blocks,
                cell_blocks,
                grain_motion,
                marker_offset,
                marker_weights,
            )
        ]
    )
    slots = lax.all_to_all(outgoing, "gx", split_axis=0, concat_axis=0, tiled=True)

    table, bonded = pl.pallas_call(
        moment_kernel,
        out_shape=[shape((6 * planes, 2 * size_z), BF16), shape((8, slab), F32)],
        in_specs=[VMEM] * 5,
        out_specs=[VMEM] * 2,
        compiler_params=params,
        cost_estimate=pl.CostEstimate(flops=20000000, bytes_accessed=4000000, transcendentals=0),
        name="moments",
    )(populations, bond_pairs, bond_rest, grain_position, grain_motion)

    pushed, filled = pl.pallas_call(
        lambda *refs: sample_kernel(*refs, size=(size_x, size_y, size_z)),
        out_shape=[
            shape((bricks, BACK_ROWS, MARKS), F32),
            shape((bricks * CAPB, MARKS), jnp.int32),
        ],
        in_specs=[VMEM] * 2,
        out_specs=[VMEM] * 2,
        compiler_params=params,
        name="sample",
    )(slots, table)
    returned = lax.all_to_all(pushed, "gx", split_axis=0, concat_axis=0, tiled=True)

    collided, *faces = pl.pallas_call(
        spread_kernel,
        out_shape=[
            shape(populations.shape, F32),
            shape((len(UP_X), size_y, size_z), F32),
            shape((len(UP_X), size_y, size_z), F32),
            shape((EDGE_ROWS, size_z), F32),
            shape((EDGE_ROWS, size_z), F32),
        ],
        in_specs=[VMEM] * 5,
        out_specs=[VMEM] * 5,
        scratch_shapes=[
            pltpu.VMEM((3 * size_z, 2 * planes), F32),
            pltpu.VMEM((5, size_x, size_y, size_z), F32),
            pltpu.SMEM((bricks * CAPB, MARKS), jnp.int32),
            pltpu.SMEM((bricks * CAPB + 1,), jnp.int32),
            pltpu.SemaphoreType.DMA,
        ],
        compiler_params=params,
        cost_estimate=pl.CostEstimate(
            flops=6000000000, bytes_accessed=8000000, transcendentals=0
        ),
        name="spread",
    )(place, slots, pushed, filled, populations)

    partial, near_face = pl.pallas_call(
        grain_kernel,
        out_shape=[shape((8, slab), F32), shape(faces[0].shape, F32)],
        in_specs=[SMEM] + [VMEM] * 4,
        out_specs=[VMEM] * 2,
        scratch_shapes=[pltpu.SMEM((bricks,), jnp.int32)],
        compiler_params=params,
        name="grain",
    )(block_dest, grain_blocks, marker_offset, returned, faces[0])
    near_x = lax.ppermute(near_face, "gx", swap("gx", 0))
    far_x = lax.ppermute(faces[1], "gx", swap("gx", 1))
    across = lax.ppermute(partial, "gy", cross(4))
    near_y, far_y, total = pl.pallas_call(
        lambda *refs: edge_kernel(*refs, size_x=size_x),
        out_shape=[
            shape((EDGE_ROWS + 8 * slab // size_z, size_z), F32),
            shape((EDGE_ROWS, size_z), F32),
            shape((8, slab), F32),
        ],
        in_specs=[VMEM] * 7,
        out_specs=[VMEM] * 3,
        compiler_params=params,
        name="edge",
    )(place, near_x, far_x, faces[2], faces[3], partial, across)
    near_y = lax.ppermute(near_y, "gy", swap("gy", 0))
    far_y = lax.ppermute(far_y, "gy", swap("gy", 1))
    total = pl.pallas_call(
        pair_kernel,
        out_shape=shape((8, slab), F32),
        in_specs=[VMEM] * 2,
        out_specs=VMEM,
        compiler_params=params,
        name="pair",
    )(total, near_y)

    populations_next = pl.pallas_call(
        stream_kernel,
        out_shape=shape(populations.shape, F32),
        in_specs=[VMEM] * 6,
        out_specs=HBM,
        scratch_shapes=[
            pltpu.VMEM(populations.shape, F32),
            pltpu.SemaphoreType.DMA((size_x,)),
        ],
        compiler_params=params,
        cost_estimate=pl.CostEstimate(flops=20000000, bytes_accessed=4000000, transcendentals=0),
        name="stream",
    )(place, collided, near_x, far_x, near_y, far_y)

    grain_load = pl.pallas_call(
        load_kernel,
        out_shape=shape((6, slab), F32),
        in_specs=[VMEM] * 3,
        out_specs=VMEM,
        compiler_params=params,
        name="load",
    )(bonded, total, lax.ppermute(total, "gy", cross(2)))
    return populations_next, grain_load


def solution(mesh):
    in_specs = (
        P(None, "gx", "gy", None),
        P(None, "gx"),
        P(None, "gx"),
        P(("gx", "gy")),
        P(None, ("gx", "gy")),
        P(None, ("gx", "gy")),
        P(("gx", "gy")),
        P(("gx", "gy")),
        P(None, "gx"),
        P(None, "gx"),
    )
    out_specs = (P(None, "gx", "gy", None), P(None, "gx"))
    return jax.shard_map(shards, mesh=mesh, in_specs=in_specs, out_specs=out_specs, check_vma=False)
```
